128 devices in a mesh: lat: 4 (over y), lon: 32 (over z, x, core).
Axes of the slice: x: 4, y: 4, z: 4, core: 2. Of those that a mesh axis runs over, the one named last changes fastest.
Arguments:
- grid_x: bfloat16 [32768, 227], P(('lat', 'lon')), may hold values from -6 to 6
- mesh_in: bfloat16 [32768, 512], P(('lat', 'lon')), may hold values from -6 to 6
- mesh_grad: bfloat16 [32768, 512], P(('lat', 'lon')), may hold values from -6 to 6
- embed_in: bfloat16 [227, 512], replicated, may hold values from -0.375 to 0.375
- enc_weights: bfloat16 [7, 512, 512], replicated, may hold values from -0.25 to 0.25
- proc_weights: bfloat16 [2, 6, 512, 512], replicated, may hold values from -0.25 to 0.25
- g2m_grid: int32 [5120], P(('lat', 'lon')), may hold values from 0 to 7
- g2m_mesh: int32 [5120], P(('lat', 'lon')), may hold values from 0 to 1023, as said below
- mesh_send: int32 [2048], P(('lat', 'lon')), may hold values from 0 to 11, as said below
- mesh_recv: int32 [2048], P(('lat', 'lon')), may hold values from 0 to 7
- halo_idx: int32 [128, 4, 1], P(('lat', 'lon')), may hold values from 0 to 7
Outputs:
- mesh_out: bfloat16 [32768, 512], P(('lat', 'lon'))
- mesh_in_grad: float32 [32768, 512], P(('lat', 'lon'))
- enc_grads: float32 [7, 512, 512], P(None, ('lat', 'lon'))
- proc_grads: float32 [2, 6, 512, 512], P(None, None, ('lat', 'lon'))
- embed_grad: float32 [227, 512], P(None, ('lat', 'lon'))
The draws below stay inside these ranges and needn't reach their ends.
Inputs may be any that keep to these rules, and one draw needn't show every extreme that they name: `g2m_mesh`: the mesh block of an edge block lies on a device with the same lat index as the edge block's device. Among one device's 40 edge blocks at most 2 name mesh blocks of any one device; in every lat row one device receives exactly 2 from every device of the row. `mesh_send`: slots below 8 are local blocks; then 1 slots each for the blocks shown by the lower-lat, upper-lat, lower-lon and upper-lon neighbour. Devices of the first lat index name no lower-lat slot, of the last none upper-lat; every other neighbour slot is named by some edge block of the device. halo_idx[d, k] lists blocks of device d shown to its neighbour k: 0 lower lat, 1 upper lat, 2 lower lon, 3 upper lon.
All inputs are finite; a program needn't handle non-finite values.
Results may differ from the reference program's by a relative error of at most 0.03.
Values may be sent and summed in bfloat16 or wider, within the bound.
A program may use at most 192 MiB of HBM per device.

```python
import jax
import jax.numpy as jnp
from jax import lax

L = 512
GV = 227
B = 32
GB_DEV = 8
MB_DEV = 8
EG_DEV = 40
EM_DEV = 16
HB = 1
ROUNDS = 2
CAP = 2
GRIDN = 32768
MESHN = 32768
G2M_BLOCKS = 5120
MESH_EDGES = 2048
N_LAT = 4
N_LON = 32


def shuffle_rows(keys, rows):

    def one_row(row_key, row_values):
        return jax.random.permutation(row_key, row_values)
    return jax.vmap(one_row)(keys, rows)


def draw_g2m_mesh(key, part):
    key = jax.random.fold_in(key, 5)
    key_hot, key_pool, key_order, key_block = jax.random.split(key, 4)
    device_count = N_LAT * N_LON
    hot_owner = jax.random.randint(key_hot, (N_LAT,), 0, N_LON)
    lat_row = jnp.arange(device_count, dtype=jnp.int32) // N_LON
    hot_dev = hot_owner[lat_row]
    owner_pool = jnp.arange((N_LON - 1) * CAP, dtype=jnp.int32) // CAP
    pools = jnp.broadcast_to(owner_pool[None, :], (device_count, (N_LON - 1) * CAP))
    shuffled = shuffle_rows(jax.random.split(key_pool, device_count), pools)
    others = shuffled[:, :EG_DEV - CAP]
    others = others + (others >= hot_dev[:, None]).astype(jnp.int32)
    owners = jnp.concatenate([jnp.broadcast_to(hot_dev[:, None], (device_count, CAP)), others], axis=1)
    owners = shuffle_rows(jax.random.split(key_order, device_count), owners)
    local_ids = jax.random.randint(key_block, (device_count, EG_DEV), 0, MB_DEV)
    block_ids = (lat_row[:, None] * N_LON + owners) * MB_DEV + local_ids
    return block_ids.reshape(-1).astype(jnp.int32)


def draw_mesh_send(key, part):
    key = jax.random.fold_in(key, 7)
    key_pick, key_order = jax.random.split(key)
    device_count = N_LAT * N_LON
    table_size = MB_DEV + 4 * HB
    picked = jax.random.randint(key_pick, (device_count, EM_DEV), 0, table_size)
    column = jnp.arange(EM_DEV, dtype=jnp.int32)[None, :]
    slots = jnp.where(column < 4 * HB, MB_DEV + column, picked)
    lat_row = (jnp.arange(device_count, dtype=jnp.int32) // N_LON)[:, None]
    low_rim = (slots >= MB_DEV) & (slots < MB_DEV + HB) & (lat_row == 0)
    high_rim = (slots >= MB_DEV + HB) & (slots < MB_DEV + 2 * HB) & (lat_row == N_LAT - 1)
    slots = jnp.where(low_rim, slots - HB, jnp.where(high_rim, slots - 2 * HB, slots))
    slots = shuffle_rows(jax.random.split(key_order, device_count), slots)
    return slots.reshape(-1).astype(jnp.int32)


def place_ends(result, stream_key, smallest, top_value):
    spot = [jax.random.randint(jax.random.fold_in(stream_key, axis), (), 0, length) for axis, length in enumerate(result.shape)]
    widest = result.shape.index(max(result.shape))
    neighbour = spot[:widest] + [(spot[widest] + 1) % result.shape[widest]] + spot[widest + 1:]
    return result.at[tuple(spot)].set(smallest).at[tuple(neighbour)].set(top_value)


def block_levels(rng, extent, shards, low, top_value):
    loudness, own = 1.0, jax.random.fold_in(rng, 6)
    for axis_at, shards_of in shards:
        steps = jnp.exp(jax.random.uniform(jax.random.fold_in(own, axis_at), (shards_of,), jnp.float32, low / len(shards), top_value / len(shards)))
        loudness = loudness * jnp.repeat(steps, extent[axis_at] // shards_of).reshape([-1 if axis == axis_at else 1 for axis in range(len(extent))])
    return loudness


def bell_draw(own_key, shape, scale, reach, pieces=(), kind=jnp.bfloat16):
    values = jax.random.normal(own_key, shape, jnp.float32) * scale
    if len(pieces) > 0:
        values = block_levels(own_key, shape, pieces, -0.22, 0.18) * values
    return jnp.clip(values, min=-reach, max=reach).astype(kind)


def setup_inputs(seed: int = 0) -> dict:
    key_list = jax.random.split(jax.random.key(seed), 12)
    return {
        "grid_x": bell_draw(key_list[0], (GRIDN, GV), 1.0, 6.0, ((0, 128),)),
        "mesh_in": bell_draw(key_list[1], (MESHN, L), 1.0, 6.0, ((0, 128),)),
        "mesh_grad": bell_draw(key_list[2], (MESHN, L), 1.0, 6.0, ((0, 128),)),
        "embed_in": bell_draw(key_list[3], (GV, L), GV ** -0.5, 0.375),
        "enc_weights": bell_draw(key_list[4], (7, L, L), L ** -0.5, 0.25),
        "proc_weights": bell_draw(key_list[5], (ROUNDS, 6, L, L), L ** -0.5, 0.25),
        "g2m_grid": place_ends(jax.random.randint(key_list[6], (G2M_BLOCKS,), 0, GB_DEV), jax.random.fold_in(key_list[6], 1), 0, GB_DEV - 1).astype(jnp.int32),
        "g2m_mesh": draw_g2m_mesh(jax.random.fold_in(key_list[11], 71), 0),
        "mesh_send": draw_mesh_send(jax.random.fold_in(key_list[11], 71), 0),
        "mesh_recv": place_ends(jax.random.randint(key_list[9], (MESH_EDGES,), 0, MB_DEV), jax.random.fold_in(key_list[9], 1), 0, MB_DEV - 1).astype(jnp.int32),
        "halo_idx": place_ends(jax.random.randint(key_list[10], (N_LAT * N_LON, 4, HB), 0, MB_DEV), jax.random.fold_in(key_list[10], 1), 0, MB_DEV - 1).astype(jnp.int32),
    }


EPSILON = 1e-05

def matmul(first_op, second_op):
    return jnp.dot(first_op, second_op, preferred_element_type=jnp.float32)

def norm_rows(values):
    average = lax.optimization_barrier(jnp.mean(values, axis=-1, keepdims=True))
    centred = values - average
    inv_std = lax.rsqrt(lax.optimization_barrier(jnp.mean(centred * centred, axis=-1, keepdims=True)) + EPSILON)
    return (centred * inv_std, inv_std)

def norm_back(grad_in, normed, inv_std):
    return inv_std * (grad_in - lax.optimization_barrier(jnp.mean(grad_in, axis=-1, keepdims=True)) - normed * lax.optimization_barrier(jnp.mean(grad_in * normed, axis=-1, keepdims=True)))

def swish_grad(values):
    sigmoid_v = jax.nn.sigmoid(values)
    return sigmoid_v * (1.0 + values * (1.0 - sigmoid_v))

def mesh_update(latent, summed, w_latent, w_summed, w_output):
    summed_bf = summed.astype(jnp.bfloat16)
    gate_in = matmul(latent, w_latent) + matmul(summed_bf, w_summed)
    hidden = jax.nn.silu(gate_in).astype(jnp.bfloat16)
    normed, inv_std = norm_rows(matmul(hidden, w_output))
    updated = (latent.astype(jnp.float32) + normed).astype(jnp.bfloat16)
    return (updated, (latent, summed_bf, gate_in, hidden, normed, inv_std))

def update_back(grad_new, cache, w_latent, w_summed, w_output):
    latent, summed_bf, gate_in, hidden, normed, inv_std = cache
    grad_out = norm_back(grad_new, normed, inv_std).astype(jnp.bfloat16)
    grad_hidden = matmul(grad_out, w_output.T)
    grad_wo = matmul(hidden.T, grad_out)
    grad_gate = (grad_hidden * swish_grad(gate_in)).astype(jnp.bfloat16)
    grad_latent = grad_new + matmul(grad_gate, w_latent.T)
    grad_summed = matmul(grad_gate, w_summed.T)
    return (grad_latent, grad_summed, matmul(latent.T, grad_gate), matmul(summed_bf.T, grad_gate), grad_wo)

def mesh_ends(mesh_send, mesh_recv, halo_idx):
    device_count = N_LAT * N_LON
    edge_device = jnp.arange(device_count * EM_DEV, dtype=jnp.int32) // EM_DEV
    lat_of = edge_device // N_LON
    lon_of = edge_device % N_LON
    is_local = mesh_send < MB_DEV
    offset = jnp.maximum(mesh_send - MB_DEV, 0)
    side_index = jnp.minimum(offset // HB, 3)
    within = offset % HB
    lat_step = jnp.where(side_index == 0, -1, jnp.where(side_index == 1, 1, 0)).astype(jnp.int32)
    lon_step = jnp.where(side_index == 2, -1, jnp.where(side_index == 3, 1, 0)).astype(jnp.int32)
    near_lat = jnp.clip(lat_of + lat_step, 0, N_LAT - 1)
    near_lon = (lon_of + lon_step) % N_LON
    near_dev = (near_lat * N_LON + near_lon).astype(jnp.int32)
    facing = jnp.array([1, 0, 3, 2], dtype=jnp.int32)[side_index]
    remote = near_dev * MB_DEV + halo_idx[near_dev, facing, within]
    sender = jnp.where(is_local, edge_device * MB_DEV + mesh_send, remote).astype(jnp.int32)
    receiver = (edge_device * MB_DEV + mesh_recv).astype(jnp.int32)
    return (sender, receiver)

def reference(grid_x, mesh_in, mesh_grad, embed_in, enc_weights, proc_weights, g2m_grid, g2m_mesh, mesh_send, mesh_recv, halo_idx):
    device_count = N_LAT * N_LON
    mesh_total = device_count * MB_DEV
    emb_pre = matmul(grid_x, embed_in)
    emb_act = jax.nn.silu(emb_pre).astype(jnp.bfloat16)
    grid_norm, grid_rstd = norm_rows(matmul(emb_act, enc_weights[0]))
    grid_lat = grid_norm.astype(jnp.bfloat16).reshape(device_count * GB_DEV, B, L)
    edge_device = jnp.arange(device_count * EG_DEV, dtype=jnp.int32) // EG_DEV
    source_block = (edge_device * GB_DEV + g2m_grid).astype(jnp.int32)
    sent_rows = grid_lat[source_block].reshape(-1, L)
    recv_proj = matmul(mesh_in, enc_weights[2]).reshape(mesh_total, B, L)
    g2m_pre = matmul(sent_rows, enc_weights[1]) + recv_proj[g2m_mesh].reshape(-1, L)
    g2m_act = jax.nn.silu(g2m_pre).astype(jnp.bfloat16)
    g2m_msg, g2m_rstd = norm_rows(matmul(g2m_act, enc_weights[3]))
    g2m_sum = jax.ops.segment_sum(g2m_msg.reshape(-1, B, L), g2m_mesh, mesh_total).reshape(-1, L)
    latent, enc_cache = mesh_update(mesh_in, g2m_sum, enc_weights[4], enc_weights[5], enc_weights[6])
    sender, receiver = mesh_ends(mesh_send, mesh_recv, halo_idx)
    caches = []
    for round_index in range(ROUNDS):
        weights = proc_weights[round_index]
        send_proj = matmul(latent, weights[0]).reshape(mesh_total, B, L)
        recv_side = matmul(latent, weights[1]).reshape(mesh_total, B, L)
        edge_pre = (send_proj[sender] + recv_side[receiver]).reshape(-1, L)
        edge_act = jax.nn.silu(edge_pre).astype(jnp.bfloat16)
        message, edge_rstd = norm_rows(matmul(edge_act, weights[2]))
        summed = jax.ops.segment_sum(message.reshape(-1, B, L), receiver, mesh_total).reshape(-1, L)
        new_latent, upd_cache = mesh_update(latent, summed, weights[3], weights[4], weights[5])
        caches.append((latent, edge_pre, edge_act, message, edge_rstd, upd_cache))
        latent = new_latent
    mesh_out = latent
    grad_h = mesh_grad.astype(jnp.float32)
    round_grads = [None] * ROUNDS
    for round_index in reversed(range(ROUNDS)):
        weights = proc_weights[round_index]
        before, edge_pre, edge_act, message, edge_rstd, upd_cache = caches[round_index]
        grad_h, grad_sum, grad_wh, grad_wa, grad_wo = update_back(grad_h, upd_cache, weights[3], weights[4], weights[5])
        grad_msg = grad_sum.reshape(mesh_total, B, L)[receiver].reshape(-1, L)
        grad_z = norm_back(grad_msg, message, edge_rstd).astype(jnp.bfloat16)
        grad_act = matmul(grad_z, weights[2].T)
        grad_we = matmul(edge_act.T, grad_z)
        grad_pre = (grad_act * swish_grad(edge_pre)).reshape(-1, B, L)
        grad_send = jax.ops.segment_sum(grad_pre, sender, mesh_total).reshape(-1, L).astype(jnp.bfloat16)
        grad_recv = jax.ops.segment_sum(grad_pre, receiver, mesh_total).reshape(-1, L).astype(jnp.bfloat16)
        grad_h = grad_h + matmul(grad_send, weights[0].T) + matmul(grad_recv, weights[1].T)
        round_grads[round_index] = jnp.stack([matmul(before.T, grad_send), matmul(before.T, grad_recv), grad_we, grad_wh, grad_wa, grad_wo])
    grad_h, grad_sum, grad_nh, grad_na, grad_n2 = update_back(grad_h, enc_cache, enc_weights[4], enc_weights[5], enc_weights[6])
    grad_msg = grad_sum.reshape(mesh_total, B, L)[g2m_mesh].reshape(-1, L)
    grad_z = norm_back(grad_msg, g2m_msg, g2m_rstd).astype(jnp.bfloat16)
    grad_act = matmul(grad_z, enc_weights[3].T)
    grad_a2 = matmul(g2m_act.T, grad_z)
    grad_pre = grad_act * swish_grad(g2m_pre)
    grad_pre_bf = grad_pre.astype(jnp.bfloat16)
    grad_as = matmul(sent_rows.T, grad_pre_bf)
    grad_recv = jax.ops.segment_sum(grad_pre.reshape(-1, B, L), g2m_mesh, mesh_total).reshape(-1, L).astype(jnp.bfloat16)
    grad_h = grad_h + matmul(grad_recv, enc_weights[2].T)
    grad_ar = matmul(mesh_in.T, grad_recv)
    grad_sent = matmul(grad_pre_bf, enc_weights[1].T).reshape(-1, B, L)
    grad_grid = jax.ops.segment_sum(grad_sent, source_block, device_count * GB_DEV).reshape(-1, L)
    grad_gz = norm_back(grad_grid, grid_norm, grid_rstd).astype(jnp.bfloat16)
    grad_e2 = matmul(emb_act.T, grad_gz)
    grad_emb = (matmul(grad_gz, enc_weights[0].T) * swish_grad(emb_pre)).astype(jnp.bfloat16)
    grad_e1 = matmul(grid_x.T, grad_emb)
    enc_grads = jnp.stack([grad_e2, grad_as, grad_ar, grad_a2, grad_nh, grad_na, grad_n2])
    return (mesh_out, grad_h, enc_grads, jnp.stack(round_grads), grad_e1)
```

```python
import functools

import jax
import jax.numpy as jnp
from jax import lax
from jax.experimental import pallas as pl
from jax.experimental.pallas import tpu as pltpu
from jax.sharding import PartitionSpec as P

B = 32
L = 512
T = 256
MB = 8
ROUNDS = 2
EPSILON = 1e-05
BF = jnp.bfloat16
F32 = jnp.float32
MESH = pl.DeviceIdType.MESH
HALF = L // 2
OPPOSITE = (1, 0, 3, 2)


def mm(a, b):
    return jnp.dot(a, b, preferred_element_type=F32)


def mt(a, b):
    return lax.dot_general(a, b, (((1,), (1,)), ((), ())), preferred_element_type=F32)


def tm(a, b):
    return lax.dot_general(a, b, (((0,), (0,)), ((), ())), preferred_element_type=F32)


def sigmoid(x):
    return 0.5 * jnp.tanh(0.5 * x) + 0.5


def swish(x):
    return x * sigmoid(x)


def swish_grad(x):
    s = sigmoid(x)
    return s * (1.0 + x * (1.0 - s))


def norm_rows(z):
    centred = z - jnp.mean(z, axis=-1, keepdims=True)
    r = lax.rsqrt(jnp.mean(centred * centred, axis=-1, keepdims=True) + EPSILON)
    return centred * r, r


def norm_back(g, y, r):
    return r * (
        g - jnp.mean(g, axis=-1, keepdims=True) - y * jnp.mean(g * y, axis=-1, keepdims=True)
    )


def iota(shape, dim):
    return lax.broadcasted_iota(jnp.int32, shape, dim)


def wide(r):
    return jnp.broadcast_to(r, (r.shape[0], 128))


def one_hot_rows(scalars, columns):
    col = iota((B, columns), 1)
    diag = (col & (B - 1)) == iota((B, columns), 0)
    block = col >> 5
    return [jnp.where(diag & (block == s), 1.0, 0.0).astype(BF) for s in scalars]


class Scatter:
    def __init__(self, cfg, where, refs, send, recv, base, rows):
        self.cfg, self.where, self.refs, self.rows = cfg, where, refs, rows
        self.send, self.recv, self.base = send, recv, base
        self.flying = []

    def copy(self, src, dst, index, device):
        c = pltpu.make_async_remote_copy(
            src_ref=src,
            dst_ref=dst,
            send_sem=self.send.at[self.base + index],
            recv_sem=self.recv.at[self.base + index],
            device_id=device,
            device_id_type=MESH,
        )
        c.start()
        self.flying.append(c)

    def wait(self):
        for c in self.flying:
            c.wait()
        self.flying = []

    def cols(self, which):
        return pl.ds(pl.multiple_of(which * HALF, HALF), HALF)

    def start_core(self):
        w = self.where
        own, crecv = self.refs.own, self.refs.crecv
        self.copy(own.at[:, :, self.cols(1 - w.core)], crecv, 0, (w.lat, w.sibling))

    def start_y(self):
        w, (ny, nz, nx) = self.where, self.cfg
        own, crecv, yrecv = self.refs.own, self.refs.crecv, self.refs.yrecv
        self.wait()
        mine = self.cols(w.core)
        step = 4

        def body(i, _):
            at = pl.ds(i * step, step)
            own[at, :, mine] = (own[at, :, mine].astype(F32) + crecv[at].astype(F32)).astype(BF)
            return 0

        lax.fori_loop(0, ny * nz * nx // step, body, 0)
        for j in range(1, ny):
            to = lax.rem(w.lat + j, ny)
            self.copy(
                own.at[pl.ds(to * nz * nx, nz * nx), :, mine],
                yrecv.at[j - 1],
                j,
                (to, w.lon),
            )

    def start_z(self):
        w, (ny, nz, nx) = self.where, self.cfg
        own, yrecv, zrecv = self.refs.own, self.refs.yrecv, self.refs.zrecv
        self.wait()
        mine = self.cols(w.core)
        base = w.lat * nz * nx

        def body(i, _):
            total = own[base + i, :, mine].astype(F32)
            for j in range(ny - 1):
                total = total + yrecv[j, i].astype(F32)
            own[base + i, :, mine] = total.astype(BF)
            return 0

        lax.fori_loop(0, nz * nx, body, 0)
        for j in range(1, nz):
            to = lax.rem(w.z + j, nz)
            self.copy(
                own.at[pl.ds(base + to * nx, nx), :, mine],
                zrecv.at[j - 1],
                ny - 1 + j,
                (w.lat, (to * nx + w.x) * 2 + w.core),
            )

    def start_x(self):
        w, (ny, nz, nx) = self.where, self.cfg
        own, zrecv, xrecv = self.refs.own, self.refs.zrecv, self.refs.xrecv
        self.wait()
        mine = self.cols(w.core)
        base = (w.lat * nz + w.z) * nx

        def body(i, _):
            total = own[base + i, :, mine].astype(F32)
            for j in range(nz - 1):
                total = total + zrecv[j, i].astype(F32)
            own[base + i, :, mine] = total.astype(BF)
            return 0

        lax.fori_loop(0, nx, body, 0)
        for j in range(1, nx):
            to = lax.rem(w.x + j, nx)
            self.copy(
                own.at[base + to, :, mine],
                xrecv.at[j - 1],
                ny - 1 + nz - 1 + j,
                (w.lat, (w.z * nx + to) * 2 + w.core),
            )

    def start_swap(self):
        w, (ny, nz, nx) = self.where, self.cfg
        own, xrecv = self.refs.own, self.refs.xrecv
        fin, swap = self.refs.fin, self.refs.swap
        self.wait()
        total = own[(w.lat * nz + w.z) * nx + w.x, :, self.cols(w.core)].astype(F32)
        for j in range(nx - 1):
            total = total + xrecv[j].astype(F32)
        fin[...] = total
        self.copy(fin, swap, ny + nz + nx - 2, (w.lat, w.sibling))

    def finish(self):
        w, (ny, nz, nx) = self.where, self.cfg
        fin, swap = self.refs.fin, self.refs.swap
        self.wait()
        per = L // (ny * nz * nx)
        mine, other = fin[...], swap[...]
        left = jnp.where(w.core == 0, mine, other)
        right = jnp.where(w.core == 0, other, mine)
        keep = []
        for k in range(self.rows // per):
            pair = []
            for side in (left, right):
                rows = side[k * per : (k + 1) * per]
                pair.append(jnp.where(w.core == 0, rows[: per // 2], rows[per // 2 :]))
            keep.append(pair)
        return keep


class Space:
    pass


def scratch_plan(cfg, n, slots, edges):
    ny, nz, nx = cfg
    chips = ny * nz * nx
    per = L // chips
    rows = slots * B
    ids = slots * 8
    v = Space()

    def vm(*shape, dtype=BF):
        return pltpu.VMEM(shape, dtype)

    v.encw = vm(7, L, L)
    v.procw = vm(ROUNDS, 6, L, L)
    v.emb_pre = vm(T, L, dtype=F32)
    v.emb_act = vm(T, L)
    v.grid_norm = vm(T, L, dtype=F32)
    v.grid_r = vm(T, 128, dtype=F32)
    v.G = vm(rows, T)
    v.sendbuf = vm(rows, L)
    v.recvbuf = vm(rows, L)
    v.backbuf = vm(rows, L)
    v.ids_send = vm(ids, 128)
    v.ids_recv = vm(ids, 128)
    v.Pm = vm(rows, T)
    v.recv_proj = vm(T, L)
    v.g_pre = vm(rows, L)
    v.g_act = vm(rows, L)
    v.g_msg = vm(rows, L)
    v.g_r = vm(rows, 128, dtype=F32)
    v.acc = vm(T, L, dtype=F32)
    v.gsum = vm(T, L)
    v.u_s = []
    v.u_gate = []
    v.u_hid = []
    v.u_y = []
    v.u_r = []
    for u in range(ROUNDS + 1):
        v.u_s.append(vm(T, L))
        v.u_gate.append(vm(T, L))
        v.u_hid.append(vm(T, L))
        v.u_y.append(vm(T, L))
        v.u_r.append(vm(T, 128, dtype=F32))
    v.dz = vm(T, L)
    v.dgate = vm(T, L)
    v.drecv = vm(T, L)
    v.dproj = vm(T, L)
    v.gh = vm(T, L, dtype=F32)
    v.Ps = vm(edges * B, T + 4 * B)
    v.Pr = vm(edges * B, T)
    v.H = vm(4 * B, T)
    v.ext = []
    v.hsend = []
    v.bsend = []
    v.brecv = []
    v.e_pre = []
    v.e_act = []
    v.e_msg = []
    v.e_r = []
    for r in range(ROUNDS):
        v.ext.append(vm(T + 4 * B, L))
        v.hsend.append(vm(4 * B, L))
        v.bsend.append(vm(4 * B, L))
        v.brecv.append(vm(4 * B, L))
        v.e_pre.append(vm(edges * B, L))
        v.e_act.append(vm(edges * B, L))
        v.e_msg.append(vm(edges * B, L))
        v.e_r.append(vm(edges * B, 128, dtype=F32))
    v.own = []
    v.crecv = []
    v.yrecv = []
    v.zrecv = []
    v.xrecv = []
    v.fin = []
    v.swap = []
    for p, count in enumerate((6, 6, 6, 2)):
        r = count * per
        v.own.append(vm(chips, r, L))
        if p < 2:
            v.crecv.append(vm(chips, r, HALF))
        v.yrecv.append(vm(ny - 1, nz * nx, r, HALF))
        v.zrecv.append(vm(nz - 1, nx, r, HALF))
        v.xrecv.append(vm(nx - 1, r, HALF))
        v.fin.append(vm(r, HALF, dtype=F32))
        v.swap.append(vm(r, HALF, dtype=F32))
    hops = ny + nz + nx - 1
    dma = pltpu.SemaphoreType.DMA
    v.w_sem = dma((2,))
    v.ids_ss, v.ids_rs = dma((n,)), dma((n,))
    v.fwd_ss, v.fwd_rs = dma((n,)), dma((n,))
    v.back_ss, v.back_rs = dma((n,)), dma((n,))
    v.halo_ss, v.halo_rs = dma((8 * ROUNDS,)), dma((8 * ROUNDS,))
    v.rs_ss, v.rs_rs = dma((4 * hops,)), dma((4 * hops,))
    return v


def leaves(plan):
    return [x for v in vars(plan).values() for x in (v if isinstance(v, list) else [v])]


def bind(plan, refs):
    rest, out = iter(refs), Space()
    for name, v in vars(plan).items():
        setattr(out, name, [next(rest) for _ in v] if isinstance(v, list) else next(rest))
    return out


def kernel(
    cfg,
    n,
    cap,
    plan,
    gx,
    mesh_in,
    mgrad,
    emb,
    encw_hbm,
    procw_hbm,
    mrow,
    mcol,
    grow,
    msend,
    mrecv,
    hidx,
    out_lat,
    out_gin,
    out_enc,
    out_proc,
    out_emb,
    *scratch,
):
    s = bind(plan, scratch)
    ny, nz, nx = cfg
    chips = ny * nz * nx
    per = L // chips
    slots = n * cap
    tiles = slots * B // T
    ppt = T // (cap * B)
    edges = msend.shape[0]
    hops = ny + nz + nx - 1

    w = Space()
    w.lat, w.lon = lax.axis_index("lat"), lax.axis_index("lon")
    w.core = lax.rem(w.lon, 2)
    w.sibling = w.lon + 1 - 2 * w.core
    w.x = lax.rem(w.lon // 2, nx)
    w.z = w.lon // (2 * nx)
    me = w.lon

    enc_copy = pltpu.make_async_copy(encw_hbm, s.encw, s.w_sem.at[0])
    proc_copy = pltpu.make_async_copy(procw_hbm, s.procw, s.w_sem.at[1])
    enc_copy.start()
    proc_copy.start()

    barrier = pltpu.get_barrier_semaphore()

    def greet(k, _):
        pl.semaphore_signal(
            barrier, inc=1, device_id=(w.lat, lax.rem(me + k, n)), device_id_type=MESH
        )
        return 0

    lax.fori_loop(1, n, greet, 0)
    for j in range(1, ny):
        pl.semaphore_signal(
            barrier, inc=1, device_id=(lax.rem(w.lat + j, ny), me), device_id_type=MESH
        )

    own_c = (mcol[...] >> 3) & (n - 1)
    own_r = (mrow[...] >> 3) & (n - 1)
    count = mrow.shape[1]
    before = (own_c == own_r) & (iota((count, count), 0) < iota((count, count), 1))
    rank = jnp.sum(jnp.where(before, 1.0, 0.0), axis=0, keepdims=True)
    slot = own_r.astype(F32) * cap + rank
    hot = iota((slots, count), 0).astype(F32) == slot
    block = jnp.sum(jnp.where(hot, grow[...].astype(F32) + 1.0, 0.0), axis=1, keepdims=True) - 1.0
    dest = (
        jnp.sum(jnp.where(hot, (mrow[...] & (MB - 1)).astype(F32) + 1.0, 0.0), axis=1, keepdims=True)
        - 1.0
    )
    spread = (iota((slots * 8, slots), 0) >> 3) == iota((slots * 8, slots), 1)
    s.ids_send[...] = mm(
        jnp.where(spread, 1.0, 0.0).astype(BF),
        jnp.broadcast_to(dest, (slots, 128)).astype(BF),
    ).astype(BF)
    pl.semaphore_wait(barrier, n - 1 + ny - 1)

    def row_copy(src, dst, size, ss, rs, to):
        return pltpu.make_async_remote_copy(
            src_ref=src.at[pl.ds(pl.multiple_of(to * size, size), size)],
            dst_ref=dst.at[pl.ds(pl.multiple_of(me * size, size), size)],
            send_sem=ss.at[to],
            recv_sem=rs.at[me],
            device_id=(w.lat, to),
            device_id_type=MESH,
        )

    def row_wait(src, dst, size, ss, rs, frm):
        return pltpu.make_async_remote_copy(
            src_ref=src.at[pl.ds(pl.multiple_of(frm * size, size), size)],
            dst_ref=dst.at[pl.ds(pl.multiple_of(frm * size, size), size)],
            send_sem=ss.at[frm],
            recv_sem=rs.at[frm],
            device_id=(w.lat, frm),
            device_id_type=MESH,
        )

    ids_args = (s.ids_send, s.ids_recv, cap * 8, s.ids_ss, s.ids_rs)
    fwd_args = (s.sendbuf, s.recvbuf, cap * B, s.fwd_ss, s.fwd_rs)
    back_args = (s.sendbuf, s.backbuf, cap * B, s.back_ss, s.back_rs)

    def send_all(args):
        def body(k, _):
            row_copy(*args, lax.rem(me + k, n)).start()
            return 0

        lax.fori_loop(1, n, body, 0)

    def sent_all(args):
        def body(k, _):
            row_wait(*args, lax.rem(me + k, n)).wait_send()
            return 0

        lax.fori_loop(1, n, body, 0)

    def keep_own(args):
        src, dst, size = args[:3]
        at = pl.ds(pl.multiple_of(me * size, size), size)
        dst[at] = src[at]

    send_all(ids_args)
    keep_own(ids_args)

    col = iota((T, T), 1)
    diag = (col & (B - 1)) == (iota((T, T), 0) & (B - 1))
    col_block = (col >> 5).astype(F32)
    block_b = jnp.broadcast_to(block, (slots, T)).astype(BF)

    def pick_grid(t, _):
        expand = ((iota((T, slots), 0) + t * T) >> 5) == iota((T, slots), 1)
        value = mm(jnp.where(expand, 1.0, 0.0).astype(BF), block_b)
        s.G[pl.ds(pl.multiple_of(t * T, T), T)] = jnp.where(
            diag & (value == col_block), 1.0, 0.0
        ).astype(BF)
        return 0

    lax.fori_loop(0, tiles, pick_grid, 0)

    emb_pre = mm(gx[...], emb[...])
    s.emb_pre[...] = emb_pre
    emb_act = swish(emb_pre).astype(BF)
    s.emb_act[...] = emb_act
    enc_copy.wait()
    encw = s.encw
    grid_norm, grid_r = norm_rows(mm(emb_act, encw[0]))
    s.grid_norm[...] = grid_norm
    s.grid_r[...] = wide(grid_r)
    s.gsum[...] = grid_norm.astype(BF)

    def fill(t, _):
        at = pl.ds(pl.multiple_of(t * T, T), T)
        s.sendbuf[at] = mm(s.G[at], s.gsum[...]).astype(BF)
        return 0

    lax.fori_loop(0, tiles, fill, 0)
    send_all(fwd_args)
    keep_own(fwd_args)

    s.recv_proj[...] = mm(mesh_in[...], encw[2]).astype(BF)
    for e in range(edges):
        (pick,) = one_hot_rows([msend[e]], T + 4 * B)
        s.Ps[pl.ds(e * B, B)] = pick
        (pick,) = one_hot_rows([mrecv[e]], T)
        s.Pr[pl.ds(e * B, B)] = pick
    for k in range(4):
        (pick,) = one_hot_rows([hidx[k]], T)
        s.H[pl.ds(k * B, B)] = pick

    def ids_wait(k, _):
        row_wait(*ids_args, lax.rem(me + k, n)).wait_recv()
        return 0

    lax.fori_loop(1, n, ids_wait, 0)
    id_rows = ppt * cap * 8
    id_pick = iota((T, id_rows), 1) == ((iota((T, id_rows), 0) >> 5) << 3)
    id_pick = jnp.where(id_pick, 1.0, 0.0).astype(BF)

    def pick_mesh(t, _):
        value = mm(id_pick, s.ids_recv[pl.ds(pl.multiple_of(t * id_rows, id_rows), id_rows)])
        value = jnp.concatenate([value, value], axis=1)
        s.Pm[pl.ds(pl.multiple_of(t * T, T), T)] = jnp.where(
            diag & (value == col_block), 1.0, 0.0
        ).astype(BF)
        return 0

    lax.fori_loop(0, tiles, pick_mesh, 0)
    s.acc[...] = jnp.zeros((T, L), F32)

    def edge_tile(i, _):
        t = lax.rem(me // ppt + tiles - i, tiles)
        for q in range(ppt):
            frm = t * ppt + q

            @pl.when(frm != me)
            def _():
                row_wait(*fwd_args, frm).wait_recv()

        at = pl.ds(pl.multiple_of(t * T, T), T)
        pick = s.Pm[at]
        pre = mm(s.recvbuf[at], encw[1]) + mm(pick, s.recv_proj[...])
        s.g_pre[at] = pre.astype(BF)
        act = swish(pre).astype(BF)
        s.g_act[at] = act
        msg, r = norm_rows(mm(act, encw[3]))
        s.g_r[at] = wide(r)
        msg = msg.astype(BF)
        s.g_msg[at] = msg
        s.acc[...] += tm(pick, msg)
        return 0

    lax.fori_loop(0, tiles, edge_tile, 0)

    def update(u, h, total, wh, wa, wo):
        sb = total.astype(BF)
        s.u_s[u][...] = sb
        gate = mm(h, wh) + mm(sb, wa)
        s.u_gate[u][...] = gate.astype(BF)
        hid = swish(gate).astype(BF)
        s.u_hid[u][...] = hid
        y, r = norm_rows(mm(hid, wo))
        s.u_y[u][...] = y.astype(BF)
        s.u_r[u][...] = wide(r)
        return (h.astype(F32) + y).astype(BF)

    def update_back(u, g, wh, wa, wo):
        dz = norm_back(g, s.u_y[u][...].astype(F32), s.u_r[u][:, :1]).astype(BF)
        s.dz[...] = dz
        dgate = (mt(dz, wo) * swish_grad(s.u_gate[u][...].astype(F32))).astype(BF)
        s.dgate[...] = dgate
        return g + mt(dgate, wh), mt(dgate, wa)

    def neighbour(k):
        if k < 2:
            return (lax.rem(w.lat + (ny - 1 if k == 0 else 1), ny), me)
        return (w.lat, lax.rem(me + (n - 1 if k == 2 else 1), n))

    def halo_copy(src, dst, offset, event, k):
        j = OPPOSITE[k]
        return pltpu.make_async_remote_copy(
            src_ref=src.at[pl.ds(k * B, B)],
            dst_ref=dst.at[pl.ds(offset + j * B, B)],
            send_sem=s.halo_ss.at[event * 4 + j],
            recv_sem=s.halo_rs.at[event * 4 + j],
            device_id=neighbour(k),
            device_id_type=MESH,
        )

    s.ext[0][pl.ds(0, T)] = update(
        0, mesh_in[...], s.acc[...], encw[4], encw[5], encw[6]
    )
    proc_copy.wait()
    procw = s.procw
    e_tiles = edges * B // T

    for r in range(ROUNDS):
        ext = s.ext[r]
        latent = ext[pl.ds(0, T)]
        s.hsend[r][...] = mm(s.H[...], latent).astype(BF)
        copies = [halo_copy(s.hsend[r], ext, T, r, k) for k in range(4)]
        for c in copies:
            c.start()
        s.gsum[...] = mm(latent, procw[r, 1]).astype(BF)
        for c in copies:
            c.wait()
        total = jnp.zeros((T, L), F32)
        for t in range(e_tiles):
            at = pl.ds(t * T, T)
            pick = s.Pr[at]
            pre = mm(mm(s.Ps[at], ext[...]).astype(BF), procw[r, 0]) + mm(pick, s.gsum[...])
            s.e_pre[r][at] = pre.astype(BF)
            act = swish(pre).astype(BF)
            s.e_act[r][at] = act
            msg, rstd = norm_rows(mm(act, procw[r, 2]))
            s.e_r[r][at] = wide(rstd)
            msg = msg.astype(BF)
            s.e_msg[r][at] = msg
            total = total + tm(pick, msg)
        new = update(r + 1, latent, total, procw[r, 3], procw[r, 4], procw[r, 5])
        if r + 1 < ROUNDS:
            s.ext[r + 1][pl.ds(0, T)] = new
        else:
            out_lat[...] = new

    parts = []
    for p, count in enumerate((6, 6, 6, 2)):
        refs = Space()
        refs.own, refs.yrecv, refs.zrecv, refs.xrecv = s.own[p], s.yrecv[p], s.zrecv[p], s.xrecv[p]
        refs.fin, refs.swap = s.fin[p], s.swap[p]
        refs.crecv = s.crecv[p % 2].at[:, pl.ds(0, count * per), :]
        parts.append(Scatter(cfg, w, refs, s.rs_ss, s.rs_rs, p * hops, count * per))

    band = L // ny
    band_chips = nz * nx

    def outer_pair(p, pair, first, second):
        own = s.own[p]

        def body(i, _):
            at = pl.ds(pl.multiple_of(i * band, band), band)
            both = []
            for a, b in (first, second):
                both.append(tm(a[:, at], b[...]).reshape(band_chips, per, b.shape[1]))
            own[pl.ds(i * band_chips, band_chips), pl.ds(pair * 2 * per, 2 * per), :] = (
                jnp.concatenate(both, axis=1).astype(BF)
            )
            return 0

        lax.fori_loop(0, ny, body, 0)

    g = mgrad[...].astype(F32)
    for r in reversed(range(ROUNDS)):
        p = ROUNDS - 1 - r
        ext = s.ext[r]
        lat_ref = ext.at[pl.ds(0, T)]
        gh, gs = update_back(r + 1, g, procw[r, 3], procw[r, 4], procw[r, 5])
        s.gh[...] = gh
        s.gsum[...] = gs.astype(BF)
        if p > 0:
            parts[p - 1].start_y()
        for t in range(e_tiles):
            at = pl.ds(t * T, T)
            gmsg = mm(s.Pr[at], s.gsum[...])
            gz = norm_back(gmsg, s.e_msg[r][at].astype(F32), s.e_r[r][at, :1]).astype(BF)
            s.e_msg[r][at] = gz
            dpre = mt(gz, procw[r, 2]) * swish_grad(s.e_pre[r][at].astype(F32))
            s.e_pre[r][at] = dpre.astype(BF)
        dpre = s.e_pre[r][...]
        gext = tm(s.Ps[...], dpre)
        s.bsend[r][...] = gext[T:].astype(BF)
        s.acc[...] = gext[:T]
        copies = [halo_copy(s.bsend[r], s.brecv[r], 0, ROUNDS + r, k) for k in range(4)]
        for c in copies:
            c.start()
        drecv = tm(s.Pr[...], dpre).astype(BF)
        s.drecv[...] = drecv
        s.gh[...] += mt(drecv, procw[r, 1])
        outer_pair(p, 0, (lat_ref, s.drecv), (s.e_act[r], s.e_msg[r]))
        outer_pair(p, 1, (lat_ref, s.dgate), (s.u_s[r + 1], s.dgate))
        for c in copies:
            c.wait()
        dproj = (s.acc[...] + tm(s.H[...], s.brecv[r][...])).astype(BF)
        s.dproj[...] = dproj
        g = s.gh[...] + mt(dproj, procw[r, 0])
        outer_pair(p, 2, (s.u_hid[r + 1], s.dz), (lat_ref, s.dproj))
        parts[p].start_core()

    gh, gs = update_back(0, g, encw[4], encw[5], encw[6])
    s.gh[...] = gh
    s.gsum[...] = gs.astype(BF)
    sent_all(ids_args)
    sent_all(fwd_args)
    s.acc[...] = jnp.zeros((T, L), F32)

    def edge_back(i, _):
        t = lax.rem(me // ppt + i, tiles)
        at = pl.ds(pl.multiple_of(t * T, T), T)
        pick = s.Pm[at]
        gmsg = mm(pick, s.gsum[...])
        gz = norm_back(gmsg, s.g_msg[at].astype(F32), s.g_r[at, :1]).astype(BF)
        s.g_msg[at] = gz
        dpre = (mt(gz, encw[3]) * swish_grad(s.g_pre[at].astype(F32))).astype(BF)
        s.g_pre[at] = dpre
        s.acc[...] += tm(pick, dpre)
        s.sendbuf[at] = mt(dpre, encw[1]).astype(BF)
        for q in range(ppt):
            to = t * ppt + q

            @pl.when(to != me)
            def _():
                row_copy(*back_args, to).start()

        return 0

    lax.fori_loop(0, tiles, edge_back, 0)
    keep_own(back_args)
    parts[1].start_y()
    drecv = s.acc[...].astype(BF)
    s.drecv[...] = drecv
    out_gin[...] = s.gh[...] + mt(drecv, encw[2])
    outer_pair(2, 0, (s.recvbuf, s.g_pre), (s.g_act, s.g_msg))
    outer_pair(2, 1, (mesh_in, s.drecv), (mesh_in, s.dgate))
    outer_pair(2, 2, (s.u_s[0], s.dgate), (s.u_hid[0], s.dz))
    parts[2].start_core()
    parts[0].start_z()
    parts[2].start_y()
    parts[0].start_x()

    s.acc[...] = jnp.zeros((T, L), F32)

    def back_tile(i, _):
        t = lax.rem(me // ppt + tiles - i, tiles)
        for q in range(ppt):
            frm = t * ppt + q

            @pl.when(frm != me)
            def _():
                row_wait(*back_args, frm).wait_recv()

        at = pl.ds(pl.multiple_of(t * T, T), T)
        s.acc[...] += tm(s.G[at], s.backbuf[at])
        return 0

    lax.fori_loop(0, tiles, back_tile, 0)
    dgz = norm_back(s.acc[...], s.grid_norm[...], s.grid_r[:, :1]).astype(BF)
    s.dz[...] = dgz
    dgpre = (mt(dgz, encw[0]) * swish_grad(s.emb_pre[...])).astype(BF)
    s.dgate[...] = dgpre

    def outer_last(i, _):
        own = s.own[3]
        at = pl.ds(pl.multiple_of(i * band, band), band)
        first = tm(s.emb_act[:, at], s.dz[...]).reshape(band_chips, per, L)
        second = tm(s.dgate[:, at], gx[...]).reshape(band_chips, per, HALF)
        second = jnp.concatenate([second, jnp.zeros((band_chips, per, HALF), F32)], axis=2)
        own[pl.ds(i * band_chips, band_chips)] = jnp.concatenate([first, second], axis=1).astype(BF)
        return 0

    lax.fori_loop(0, ny, outer_last, 0)
    parts[3].start_core()
    parts[1].start_z()
    parts[0].start_swap()
    parts[3].start_y()
    parts[2].start_z()
    parts[1].start_x()
    parts[3].start_z()
    parts[2].start_x()
    parts[1].start_swap()
    parts[3].start_x()
    parts[2].start_swap()
    parts[3].start_swap()
    sent_all(back_args)

    left, right = pl.ds(0, HALF), pl.ds(HALF, HALF)
    for p in range(ROUNDS):
        for k, (a, b) in zip((1, 2, 3, 4, 5, 0), parts[p].finish()):
            out_proc[ROUNDS - 1 - p, k, :, left] = a
            out_proc[ROUNDS - 1 - p, k, :, right] = b
    for k, (a, b) in zip((1, 3, 2, 4, 5, 6), parts[2].finish()):
        out_enc[k, :, left] = a
        out_enc[k, :, right] = b
    last = parts[3].finish()
    out_enc[0, :, left], out_enc[0, :, right] = last[0]
    out_emb[...] = last[1][0]


def on_device(
    cfg,
    grid_x,
    mesh_in,
    mesh_grad,
    embed_in,
    enc_weights,
    proc_weights,
    g2m_grid,
    g2m_mesh,
    mesh_send,
    mesh_recv,
    halo_idx,
):
    n = lax.axis_size("lon")
    count = g2m_grid.shape[0]
    cap = (count + n - 1) // n
    variables = grid_x.shape[1]
    chips = cfg[0] * cfg[1] * cfg[2]
    mine = L // chips // 2
    gx = jnp.pad(grid_x, ((0, 0), (0, HALF - variables)))
    emb = jnp.pad(embed_in, ((0, HALF - variables), (0, 0)))
    plan = scratch_plan(cfg, n, n * cap, mesh_send.shape[0])
    vmem = pl.BlockSpec(memory_space=pltpu.VMEM)
    smem = pl.BlockSpec(memory_space=pltpu.SMEM)
    hbm = pl.BlockSpec(memory_space=pl.ANY)
    latent, grad_in, enc, proc, emb_t = pl.pallas_call(
        functools.partial(kernel, cfg, n, cap, plan),
        out_shape=(
            jax.ShapeDtypeStruct((T, L), BF),
            jax.ShapeDtypeStruct((T, L), F32),
            jax.ShapeDtypeStruct((7, mine, L), F32),
            jax.ShapeDtypeStruct((ROUNDS, 6, mine, L), F32),
            jax.ShapeDtypeStruct((mine, HALF), F32),
        ),
        in_specs=[vmem] * 4 + [hbm] * 2 + [vmem] * 3 + [smem] * 3,
        out_specs=(vmem,) * 5,
        scratch_shapes=leaves(plan),
        compiler_params=pltpu.CompilerParams(
            collective_id=0, has_side_effects=True, vmem_limit_bytes=62 * 1024 * 1024
        ),
    )(
        gx,
        mesh_in,
        mesh_grad,
        emb,
        enc_weights,
        proc_weights,
        g2m_mesh.reshape(1, count),
        g2m_mesh.reshape(count, 1),
        g2m_grid.reshape(1, count),
        mesh_send,
        mesh_recv,
        halo_idx.reshape(4),
    )
    return latent, grad_in, enc, proc, emb_t[:, :variables].T


def solution(mesh):
    n = mesh.shape["lon"]
    nx = 4 if n == 32 else 2
    cfg = (mesh.shape["lat"], n // (2 * nx), nx)
    return jax.shard_map(
        functools.partial(on_device, cfg),
        mesh=mesh,
        in_specs=(
            P(("lat", "lon"), None),
            P(("lat", "lon"), None),
            P(("lat", "lon"), None),
            P(),
            P(),
            P(),
            P(("lat", "lon")),
            P(("lat", "lon")),
            P(("lat", "lon")),
            P(("lat", "lon")),
            P(("lat", "lon"), None, None),
        ),
        out_specs=(
            P(("lat", "lon"), None),
            P(("lat", "lon"), None),
            P(None, ("lat", "lon"), None),
            P(None, None, ("lat", "lon"), None),
            P(None, ("lat", "lon")),
        ),
        check_vma=False,
    )
```

```python
import functools

import jax
import jax.numpy as jnp
from jax import lax
from jax.experimental import pallas as pl
from jax.experimental.pallas import tpu as pltpu
from jax.sharding import PartitionSpec as P

B = 32
L = 512
T = 256
MB = 8
ROUNDS = 2
EPSILON = 1e-05
BF = jnp.bfloat16
F32 = jnp.float32
MESH = pl.DeviceIdType.MESH
HALF = L // 2
OPPOSITE = (1, 0, 3, 2)
STRIDE = 19


def mm(a, b):
    return jnp.dot(a, b, preferred_element_type=F32)


def mt(a, b):
    return lax.dot_general(a, b, (((1,), (1,)), ((), ())), preferred_element_type=F32)


def tm(a, b):
    return lax.dot_general(a, b, (((0,), (0,)), ((), ())), preferred_element_type=F32)


def sigmoid(x):
    return 0.5 * jnp.tanh(0.5 * x) + 0.5


def swish(x):
    return x * sigmoid(x)


def swish_grad(x):
    s = sigmoid(x)
    return s * (1.0 + x * (1.0 - s))


def norm_rows(z):
    centred = z - jnp.mean(z, axis=-1, keepdims=True)
    r = lax.rsqrt(jnp.mean(centred * centred, axis=-1, keepdims=True) + EPSILON)
    return centred * r, r


def norm_back(g, y, r):
    return r * (
        g - jnp.mean(g, axis=-1, keepdims=True) - y * jnp.mean(g * y, axis=-1, keepdims=True)
    )


def iota(shape, dim):
    return lax.broadcasted_iota(jnp.int32, shape, dim)


def wide(r):
    return jnp.broadcast_to(r, (r.shape[0], 128))


class Group:
    def __init__(self, cfg, w, refs, sems, base, rows):
        self.cfg, self.w, self.refs, self.rows = cfg, w, refs, rows
        self.send, self.recv = sems
        self.base = base
        self.lanes = []

    def copy(self, src, dst, index, device):
        c = pltpu.make_async_remote_copy(
            src_ref=src,
            dst_ref=dst,
            send_sem=self.send.at[index],
            recv_sem=self.recv.at[index],
            device_id=device,
            device_id_type=MESH,
        )
        c.start()
        return c

    def half(self, which):
        return pl.ds(pl.multiple_of(which * HALF, HALF), HALF)

    def start_core(self):
        w = self.w
        src = self.refs.own.at[:, :, :, :, self.half(1 - w.core)]
        self.core = self.copy(src, self.refs.crecv, self.base, (w.lat, w.sibling))

    def add_core(self):
        own, crecv = self.refs.own, self.refs.crecv
        mine = self.half(self.w.core)
        ny, nz, _ = self.cfg
        self.core.wait()

        def body(y, _):
            for z in range(nz):
                total = own[y, z, :, :, mine].astype(F32) + crecv[y, z].astype(F32)
                own[y, z, :, :, mine] = total.astype(BF)
            return 0

        lax.fori_loop(0, ny, body, 0)

    def step(self):
        for lane in self.lanes:
            lane.step()

    def start_swap(self):
        w = self.w
        self.step()
        self.swapped = self.copy(
            self.refs.fin, self.refs.swap, self.base + 1, (w.lat, w.sibling)
        )

    def finish(self):
        w, (ny, nz, nx) = self.w, self.cfg
        self.swapped.wait()
        per = L // (ny * nz * nx)
        mine, other = self.refs.fin[...], self.refs.swap[...]
        left = jnp.where(w.core == 0, mine, other)
        right = jnp.where(w.core == 0, other, mine)
        keep = []
        for k in range(self.rows // per):
            pair = []
            for side in (left, right):
                rows = side[k * per : (k + 1) * per]
                pair.append(jnp.where(w.core == 0, rows[: per // 2], rows[per // 2 :]))
            keep.append(pair)
        return keep


class Lane:
    def __init__(self, group, recvs, base, rows, cols, order):
        self.group, self.recvs, self.base = group, recvs, base
        self.rows, self.cols, self.order = rows, cols, order
        w = group.w
        self.at = (w.lat, w.z, w.x)
        self.fixed = [slice(None)] * 3
        self.stage = 0
        self.flying = []

    def index(self, fixed):
        start = pl.multiple_of(self.group.w.core * HALF + self.cols[0], 128)
        return tuple(fixed) + (pl.ds(*self.rows), pl.ds(start, self.cols[1]))

    def device(self, axis, to):
        y, z, x = [to if a == axis else c for a, c in enumerate(self.at)]
        return (y, (z * self.group.cfg[2] + x) * 2 + self.group.w.core)

    def step(self):
        if self.stage > 0:
            self.collect()
        if self.stage < 3:
            self.launch()
        self.stage += 1

    def launch(self):
        axis, own = self.order[self.stage], self.group.refs.own
        size = self.group.cfg[axis]
        for j in range(1, size):
            to = lax.rem(self.at[axis] + j, size)
            there = list(self.fixed)
            there[axis] = to
            self.flying.append(
                self.group.copy(
                    own.at[self.index(there)],
                    self.recvs[self.stage].at[j - 1],
                    self.base,
                    self.device(axis, to),
                )
            )
            self.base += 1
        self.fixed[axis] = self.at[axis]

    def collect(self):
        own, recv = self.group.refs.own, self.recvs[self.stage - 1]
        for c in self.flying:
            c.wait()
        self.flying = []
        peers = recv.shape[0]
        free = [a for a in range(3) if isinstance(self.fixed[a], slice)]
        if not free:
            total = own[self.index(self.fixed)].astype(F32)
            for j in range(peers):
                total = total + recv[j].astype(F32)
            self.group.refs.fin[pl.ds(*self.rows), pl.ds(*self.cols)] = total
            return
        for i in range(self.group.cfg[free[0]]):
            here = list(self.fixed)
            here[free[0]] = i
            total = own[self.index(here)].astype(F32)
            for j in range(peers):
                total = total + recv[j, i].astype(F32)
            own[self.index(here)] = total.astype(BF)


class Space:
    pass


Y, Z, X = 0, 1, 2
GROUPS = (
    (6, ((0, 1, 0, HALF, (Y, Z, X)), (1, 1, 0, HALF, (Z, X, Y)), (2, 1, 0, HALF, (X, Y, Z)))),
    (6, ((0, 3, 0, HALF, (Y, Z, X)),)),
    (6, ((0, 1, 0, HALF, (Y, Z, X)), (1, 1, 0, HALF, (Z, X, Y)), (2, 1, 0, HALF, (X, Y, Z)))),
    (2, ((0, 1, 0, 128, (Y, Z, X)), (0, 1, 128, 128, (Z, X, Y)))),
)


def scratch_plan(cfg, n, slots, edges):
    ny, nz, nx = cfg
    per = L // (ny * nz * nx)
    rows = slots * B
    ids = slots * 8
    v = Space()

    def vm(*shape, dtype=BF):
        return pltpu.VMEM(shape, dtype)

    v.encw = vm(7, L, L)
    v.procw = vm(ROUNDS, 6, L, L)
    v.gxp = vm(HALF, T)
    v.emb_pre = vm(T, L)
    v.emb_act = vm(T, L)
    v.grid_norm = vm(T, L)
    v.grid_r = vm(T, 128, dtype=F32)
    v.G = vm(rows, T)
    v.sendbuf = vm(rows, L)
    v.recvbuf = vm(rows, L)
    v.backbuf = vm(rows, L)
    v.ids_send = vm(ids, 128)
    v.ids_recv = vm(ids, 128)
    v.Pm = vm(rows, T)
    v.recv_proj = vm(T, L)
    v.g_pre = vm(rows, L)
    v.g_act = vm(rows, L)
    v.g_msg = vm(rows, L)
    v.g_r = vm(rows, 128)
    v.acc = vm(T, L, dtype=F32)
    v.gsum = vm(T, L)
    v.u_s, v.u_gate, v.u_hid, v.u_y, v.u_r = [], [], [], [], []
    for u in range(ROUNDS + 1):
        v.u_s.append(vm(T, L))
        v.u_gate.append(vm(T, L))
        v.u_hid.append(vm(T, L))
        v.u_y.append(vm(T, L))
        v.u_r.append(vm(T, 128, dtype=F32))
    v.dz = vm(T, L)
    v.dgate = vm(T, L)
    v.drecv = vm(T, L)
    v.Pc = vm(edges * B, 2 * T)
    v.Ph = vm(edges * B, 4 * B)
    v.H = vm(4 * B, T)
    v.lat, v.halo, v.hsend, v.bsend, v.brecv = [], [], [], [], []
    v.e_pre, v.e_act, v.e_msg, v.e_r = [], [], [], []
    for r in range(ROUNDS):
        v.lat.append(vm(T, L))
        v.halo.append(vm(4 * B, L))
        v.hsend.append(vm(4 * B, L))
        v.bsend.append(vm(4 * B, L))
        v.brecv.append(vm(4 * B, L))
        v.e_pre.append(vm(edges * B, L))
        v.e_act.append(vm(edges * B, L))
        v.e_msg.append(vm(edges * B, L))
        v.e_r.append(vm(edges * B, 128, dtype=F32))
    v.own, v.crecv, v.fin, v.swap, v.lanes = [], [], [], [], []
    sems = 0
    for p, (count, lanes) in enumerate(GROUPS):
        r = count * per
        v.own.append(vm(*cfg, r, L))
        if p < 2:
            v.crecv.append(vm(*cfg, r, HALF))
        v.fin.append(vm(r, HALF, dtype=F32))
        v.swap.append(vm(r, HALF, dtype=F32))
        sems += 2
        for _, some, _, width, order in lanes:
            left = [0, 1, 2]
            for axis in order:
                left.remove(axis)
                free = [cfg[a] for a in left]
                v.lanes.append(vm(cfg[axis] - 1, *free, some * 2 * per, width))
                sems += cfg[axis] - 1
    dma = pltpu.SemaphoreType.DMA
    v.w_sem = dma((2,))
    v.ids_ss, v.ids_rs = dma((n,)), dma((n,))
    v.fwd_ss, v.fwd_rs = dma((n,)), dma((n,))
    v.back_ss, v.back_rs = dma((n,)), dma((n,))
    v.halo_ss, v.halo_rs = dma((8 * ROUNDS,)), dma((8 * ROUNDS,))
    v.rs_ss, v.rs_rs = dma((sems,)), dma((sems,))
    return v


def leaves(plan):
    return [x for v in vars(plan).values() for x in (v if isinstance(v, list) else [v])]


def bind(plan, refs):
    rest, out = iter(refs), Space()
    for name, v in vars(plan).items():
        setattr(out, name, [next(rest) for _ in v] if isinstance(v, list) else next(rest))
    return out


def kernel(
    cfg,
    n,
    cap,
    plan,
    gxt,
    mesh_in,
    mgrad,
    emb,
    encw_hbm,
    procw_hbm,
    mrow,
    grow,
    msend,
    mrecv,
    hidx,
    out_lat,
    out_gin,
    out_enc,
    out_proc,
    out_emb,
    *scratch,
):
    s = bind(plan, scratch)
    ny, nz, nx = cfg
    per = L // (ny * nz * nx)
    slots = n * cap
    tiles = slots * B // T
    ppt = T // (cap * B)
    edges = msend.shape[0]
    variables = gxt.shape[0]

    w = Space()
    w.lat, w.lon = lax.axis_index("lat"), lax.axis_index("lon")
    w.core = lax.rem(w.lon, 2)
    w.sibling = w.lon + 1 - 2 * w.core
    w.x = lax.rem(w.lon // 2, nx)
    w.z = w.lon // (2 * nx)
    me = w.lon

    enc_copy = pltpu.make_async_copy(encw_hbm, s.encw, s.w_sem.at[0])
    proc_copy = pltpu.make_async_copy(procw_hbm, s.procw, s.w_sem.at[1])
    enc_copy.start()
    proc_copy.start()

    barrier = pltpu.get_barrier_semaphore()

    def greet(k, _):
        pl.semaphore_signal(
            barrier, inc=1, device_id=(w.lat, lax.rem(me + k, n)), device_id_type=MESH
        )
        return 0

    lax.fori_loop(1, n, greet, 0)
    for j in range(1, ny):
        pl.semaphore_signal(
            barrier, inc=1, device_id=(lax.rem(w.lat + j, ny), me), device_id_type=MESH
        )

    count = mrow.shape[1]
    owner = (mrow[...] >> 3) & (n - 1)
    owner_hot = jnp.where(iota((n, count), 0) == owner, 1.0, 0.0)
    same = tm(owner_hot.astype(BF), owner_hot.astype(BF))
    before = iota((count, count), 0) < iota((count, count), 1)
    rank = jnp.sum(jnp.where(before, same, 0.0), axis=0, keepdims=True)
    far_z = (owner // (2 * nx) + nz - w.z) & (nz - 1)
    far_x = ((owner // 2) & (nx - 1)) + nx - w.x & (nx - 1)
    far = (far_z * nx + far_x) * 2 + ((owner + w.core) & 1)
    place_of = (far * pow(STRIDE, -1, n) + n - 1) & (n - 1)
    slot = place_of.astype(F32) * cap + rank
    hot = iota((slots, count), 0).astype(F32) == slot
    block = jnp.sum(jnp.where(hot, grow[...].astype(F32) + 1.0, 0.0), axis=1, keepdims=True) - 1.0
    dest = (
        jnp.sum(jnp.where(hot, (mrow[...] & (MB - 1)).astype(F32) + 1.0, 0.0), axis=1, keepdims=True)
        - 1.0
    )
    spread = (iota((slots * 8, slots), 0) >> 3) == iota((slots * 8, slots), 1)
    s.ids_send[...] = mm(
        jnp.where(spread, 1.0, 0.0).astype(BF),
        jnp.broadcast_to(dest, (slots, 128)).astype(BF),
    ).astype(BF)

    def at_offset(p, sign):
        q = lax.rem(STRIDE * (p + 1), n)
        z = lax.rem(w.z + nz + sign * (q // (2 * nx)), nz)
        x = lax.rem(w.x + nx + sign * lax.rem(q // 2, nx), nx)
        return (z * nx + x) * 2 + lax.rem(w.core + lax.rem(q, 2), 2)

    def row_copy(src, dst, size, ss, rs, sign, p):
        at = pl.ds(pl.multiple_of(p * size, size), size)
        return pltpu.make_async_remote_copy(
            src_ref=src.at[at],
            dst_ref=dst.at[at],
            send_sem=ss.at[p],
            recv_sem=rs.at[p],
            device_id=(w.lat, at_offset(p, sign)),
            device_id_type=MESH,
        )

    ids_args = (s.ids_send, s.ids_recv, cap * 8, s.ids_ss, s.ids_rs, 1)
    fwd_args = (s.sendbuf, s.recvbuf, cap * B, s.fwd_ss, s.fwd_rs, 1)
    back_args = (s.sendbuf, s.backbuf, cap * B, s.back_ss, s.back_rs, -1)

    def send_all(args):
        def body(p, _):
            row_copy(*args, p).start()
            return 0

        lax.fori_loop(0, n - 1, body, 0)

    def sent_all(args):
        def body(p, _):
            row_copy(*args, p).wait_send()
            return 0

        lax.fori_loop(0, n - 1, body, 0)

    def keep_own(args):
        src, dst, size = args[:3]
        at = pl.ds((n - 1) * size, size)
        dst[at] = src[at]

    s.gxp[...] = jnp.zeros((HALF, T), BF)
    s.gxp[pl.ds(0, variables), :] = gxt[...]
    embp = s.sendbuf.at[pl.ds(0, HALF)]
    embp[...] = jnp.zeros((HALF, L), BF)
    embp[pl.ds(0, variables), :] = emb[...]
    emb_pre = tm(s.gxp[...], embp[...])
    s.emb_pre[...] = emb_pre.astype(BF)
    emb_act = swish(emb_pre).astype(BF)
    s.emb_act[...] = emb_act
    enc_copy.wait()
    encw = s.encw
    grid_norm, grid_r = norm_rows(mm(emb_act, encw[0]))
    s.grid_norm[...] = grid_norm.astype(BF)
    s.grid_r[...] = wide(grid_r)

    pl.semaphore_wait(barrier, n - 1 + ny - 1)
    send_all(ids_args)

    col = iota((T, T), 1)
    diag = (col & (B - 1)) == (iota((T, T), 0) & (B - 1))
    col_block = (col >> 5).astype(F32)
    block_b = jnp.broadcast_to(block, (slots, T)).astype(BF)

    def fill(t, _):
        at = pl.ds(pl.multiple_of(t * T, T), T)
        expand = ((iota((T, slots), 0) + t * T) >> 5) == iota((T, slots), 1)
        value = mm(jnp.where(expand, 1.0, 0.0).astype(BF), block_b)
        pick = jnp.where(diag & (value == col_block), 1.0, 0.0).astype(BF)
        s.G[at] = pick
        s.sendbuf[at] = mm(pick, s.grid_norm[...]).astype(BF)
        for q in range(ppt):
            p = t * ppt + q

            @pl.when(p < n - 1)
            def _():
                row_copy(*fwd_args, p).start()

        return 0

    lax.fori_loop(0, tiles, fill, 0)
    keep_own(ids_args)
    keep_own(fwd_args)

    s.recv_proj[...] = mm(mesh_in[...], encw[2]).astype(BF)

    def place(columns):
        col = iota((B, columns), 1)
        return (col & (B - 1)) == iota((B, columns), 0), col >> 5

    diag_c, block_c = place(2 * T)
    diag_h, block_h = place(4 * B)
    diag_l, block_l = place(T)
    for e in range(edges):
        sender = msend[e]
        local = jnp.where(sender < MB, sender, -1)
        hit = (block_c == local) | (block_c == mrecv[e] + MB)
        s.Pc[pl.ds(e * B, B)] = jnp.where(diag_c & hit, 1.0, 0.0).astype(BF)
        s.Ph[pl.ds(e * B, B)] = jnp.where(diag_h & (block_h == sender - MB), 1.0, 0.0).astype(BF)
    for k in range(4):
        s.H[pl.ds(k * B, B)] = jnp.where(diag_l & (block_l == hidx[k]), 1.0, 0.0).astype(BF)

    def ids_wait(p, _):
        row_copy(*ids_args, p).wait_recv()
        return 0

    lax.fori_loop(0, n - 1, ids_wait, 0)
    id_rows = ppt * cap * 8
    id_pick = iota((T, id_rows), 1) == ((iota((T, id_rows), 0) >> 5) << 3)
    id_pick = jnp.where(id_pick, 1.0, 0.0).astype(BF)

    def pick_mesh(t, _):
        value = mm(id_pick, s.ids_recv[pl.ds(pl.multiple_of(t * id_rows, id_rows), id_rows)])
        value = jnp.concatenate([value, value], axis=1)
        s.Pm[pl.ds(pl.multiple_of(t * T, T), T)] = jnp.where(
            diag & (value == col_block), 1.0, 0.0
        ).astype(BF)
        return 0

    lax.fori_loop(0, tiles, pick_mesh, 0)
    s.acc[...] = jnp.zeros((T, L), F32)

    def edge_tile(t, _):
        for q in range(ppt):
            p = t * ppt + q

            @pl.when(p < n - 1)
            def _():
                row_copy(*fwd_args, p).wait_recv()

        at = pl.ds(pl.multiple_of(t * T, T), T)
        pick = s.Pm[at]
        pre = mm(s.recvbuf[at], encw[1]) + mm(pick, s.recv_proj[...])
        s.g_pre[at] = pre.astype(BF)
        act = swish(pre).astype(BF)
        s.g_act[at] = act
        msg, r = norm_rows(mm(act, encw[3]))
        s.g_r[at] = wide(r).astype(BF)
        msg = msg.astype(BF)
        s.g_msg[at] = msg
        s.acc[...] += tm(pick, msg)
        return 0

    lax.fori_loop(0, tiles, edge_tile, 0)

    def update(u, h, total, wh, wa, wo):
        sb = total.astype(BF)
        s.u_s[u][...] = sb
        gate = mm(h, wh) + mm(sb, wa)
        s.u_gate[u][...] = gate.astype(BF)
        hid = swish(gate).astype(BF)
        s.u_hid[u][...] = hid
        y, r = norm_rows(mm(hid, wo))
        s.u_y[u][...] = y.astype(BF)
        s.u_r[u][...] = wide(r)
        return (h.astype(F32) + y).astype(BF)

    def update_back(u, wh, wa, wo):
        dz = norm_back(out_gin[...], s.u_y[u][...].astype(F32), s.u_r[u][:, :1]).astype(BF)
        s.dz[...] = dz
        dgate = (mt(dz, wo) * swish_grad(s.u_gate[u][...].astype(F32))).astype(BF)
        s.dgate[...] = dgate
        out_gin[...] += mt(dgate, wh)
        return mt(dgate, wa)

    def neighbour(k):
        if k < 2:
            return (lax.rem(w.lat + (ny - 1 if k == 0 else 1), ny), me)
        return (w.lat, lax.rem(me + (n - 1 if k == 2 else 1), n))

    def halo_copy(src, dst, event, k):
        j = OPPOSITE[k]
        return pltpu.make_async_remote_copy(
            src_ref=src.at[pl.ds(k * B, B)],
            dst_ref=dst.at[pl.ds(j * B, B)],
            send_sem=s.halo_ss.at[event * 4 + j],
            recv_sem=s.halo_rs.at[event * 4 + j],
            device_id=neighbour(k),
            device_id_type=MESH,
        )

    s.lat[0][...] = update(0, mesh_in[...], s.acc[...], encw[4], encw[5], encw[6])
    proc_copy.wait()
    procw = s.procw
    top, bottom = pl.ds(0, T), pl.ds(T, T)
    sent_all(ids_args)
    sent_all(fwd_args)
    proj = s.sendbuf.at[pl.ds(0, 2 * T)]
    mixed = s.sendbuf.at[pl.ds(4 * T, 2 * T)]

    for r in range(ROUNDS):
        latent = s.lat[r][...]
        s.hsend[r][...] = mm(s.H[...], latent).astype(BF)
        copies = [halo_copy(s.hsend[r], s.halo[r], r, k) for k in range(4)]
        for c in copies:
            c.start()
        proj[top] = mm(latent, procw[r, 0]).astype(BF)
        proj[bottom] = mm(latent, procw[r, 1]).astype(BF)
        mixed[...] = mm(s.Pc[...], proj[...]).astype(BF)
        for c in copies:
            c.wait()
        shown = mm(s.halo[r][...], procw[r, 0]).astype(BF)
        pre = mixed[...].astype(F32) + mm(s.Ph[...], shown)
        s.e_pre[r][...] = pre.astype(BF)
        act = swish(pre).astype(BF)
        s.e_act[r][...] = act
        msg, rstd = norm_rows(mm(act, procw[r, 2]))
        s.e_r[r][...] = wide(rstd)
        msg = msg.astype(BF)
        s.e_msg[r][...] = msg
        total = tm(s.Pc[:, bottom], msg)
        new = update(r + 1, latent, total, procw[r, 3], procw[r, 4], procw[r, 5])
        if r + 1 < ROUNDS:
            s.lat[r + 1][...] = new
        else:
            out_lat[...] = new

    dproj_ref = s.sendbuf.at[pl.ds(2 * T, T)]
    groups = []
    sem = lane_at = 0
    for p, (count, lanes) in enumerate(GROUPS):
        refs = Space()
        refs.own, refs.fin, refs.swap = s.own[p], s.fin[p], s.swap[p]
        refs.crecv = s.crecv[p % 2].at[:, :, :, pl.ds(0, count * per), :]
        group = Group(cfg, w, refs, (s.rs_ss, s.rs_rs), sem, count * per)
        sem += 2
        for first, some, left, width, order in lanes:
            rows = (first * 2 * per, some * 2 * per)
            recvs = s.lanes[lane_at : lane_at + 3]
            group.lanes.append(Lane(group, recvs, sem, rows, (left, width), order))
            lane_at += 3
            sem += ny + nz + nx - 3
        groups.append(group)

    def outer_pair(p, pair, first, second):
        band = L // ny
        for y in range(ny):
            at = pl.ds(y * band, band)
            both = [tm(a[:, at], b[...]).reshape(nz, nx, per, L) for a, b in (first, second)]
            rows = pl.ds(pair * 2 * per, 2 * per)
            s.own[p][y, :, :, rows, :] = jnp.concatenate(both, axis=2).astype(BF)

    out_gin[...] = mgrad[...].astype(F32)
    for r in reversed(range(ROUNDS)):
        p = ROUNDS - 1 - r
        gs = update_back(r + 1, procw[r, 3], procw[r, 4], procw[r, 5])
        gmsg = mm(s.Pc[:, bottom], gs.astype(BF))
        gz = norm_back(gmsg, s.e_msg[r][...].astype(F32), s.e_r[r][:, :1]).astype(BF)
        s.e_msg[r][...] = gz
        dpre = (mt(gz, procw[r, 2]) * swish_grad(s.e_pre[r][...].astype(F32))).astype(BF)
        s.e_pre[r][...] = dpre
        s.bsend[r][...] = tm(s.Ph[...], dpre).astype(BF)
        copies = [halo_copy(s.bsend[r], s.brecv[r], ROUNDS + r, k) for k in range(4)]
        for c in copies:
            c.start()
        mixed[...] = tm(s.Pc[...], s.e_pre[r][...]).astype(BF)
        drecv = mixed[bottom]
        s.drecv[...] = drecv
        out_gin[...] += mt(drecv, procw[r, 1])
        outer_pair(p, 0, (s.lat[r], s.drecv), (s.e_act[r], s.e_msg[r]))
        outer_pair(p, 1, (s.lat[r], s.dgate), (s.u_s[r + 1], s.dgate))
        if p > 0:
            groups[p - 1].add_core()
            groups[p - 1].step()
        for c in copies:
            c.wait()
        dproj = (mixed[top].astype(F32) + tm(s.H[...], s.brecv[r][...])).astype(BF)
        dproj_ref[...] = dproj
        out_gin[...] += mt(dproj, procw[r, 0])
        outer_pair(p, 2, (s.u_hid[r + 1], s.dz), (s.lat[r], dproj_ref))
        groups[p].start_core()

    gs = update_back(0, encw[4], encw[5], encw[6])
    s.gsum[...] = gs.astype(BF)
    s.acc[...] = jnp.zeros((T, L), F32)

    def edge_back(t, _):
        at = pl.ds(pl.multiple_of(t * T, T), T)
        pick = s.Pm[at]
        gmsg = mm(pick, s.gsum[...])
        gz = norm_back(gmsg, s.g_msg[at].astype(F32), s.g_r[at, :1].astype(F32)).astype(BF)
        s.g_msg[at] = gz
        dpre = (mt(gz, encw[3]) * swish_grad(s.g_pre[at].astype(F32))).astype(BF)
        s.g_pre[at] = dpre
        s.acc[...] += tm(pick, dpre)
        s.sendbuf[at] = mt(dpre, encw[1]).astype(BF)
        for q in range(ppt):
            p = t * ppt + q

            @pl.when(p < n - 1)
            def _():
                row_copy(*back_args, p).start()

        return 0

    lax.fori_loop(0, tiles // 2, edge_back, 0)
    groups[1].add_core()
    groups[1].step()
    lax.fori_loop(tiles // 2, tiles, edge_back, 0)
    keep_own(back_args)
    groups[0].step()
    drecv = s.acc[...].astype(BF)
    s.drecv[...] = drecv
    out_gin[...] += mt(drecv, encw[2])
    outer_pair(2, 0, (s.recvbuf, s.g_pre), (s.g_act, s.g_msg))
    outer_pair(2, 1, (mesh_in, s.drecv), (mesh_in, s.dgate))
    outer_pair(2, 2, (s.u_s[0], s.dgate), (s.u_hid[0], s.dz))
    groups[2].start_core()
    groups[0].step()

    s.acc[...] = jnp.zeros((T, L), F32)

    def back_tile(t, _):
        for q in range(ppt):
            p = t * ppt + q

            @pl.when(p < n - 1)
            def _():
                row_copy(*back_args, p).wait_recv()

        at = pl.ds(pl.multiple_of(t * T, T), T)
        s.acc[...] += tm(s.G[at], s.backbuf[at])
        return 0

    lax.fori_loop(0, tiles // 2, back_tile, 0)
    groups[2].add_core()
    groups[1].step()
    lax.fori_loop(tiles // 2, tiles, back_tile, 0)
    groups[2].step()
    dgz = norm_back(s.acc[...], s.grid_norm[...].astype(F32), s.grid_r[:, :1]).astype(BF)
    dgpre = (mt(dgz, encw[0]) * swish_grad(s.emb_pre[...].astype(F32))).astype(BF)
    first = tm(s.emb_act[...], dgz).reshape(ny, nz, nx, per, L)
    second = mm(s.gxp[...], dgpre).T.reshape(ny, nz, nx, per, HALF)
    second = jnp.concatenate([second, jnp.zeros_like(second)], axis=4)
    s.own[3][...] = jnp.concatenate([first, second], axis=3).astype(BF)
    groups[3].start_core()
    groups[0].start_swap()
    groups[1].step()
    groups[3].add_core()
    groups[3].step()
    groups[2].step()
    groups[1].start_swap()
    groups[3].step()
    groups[2].step()
    groups[3].step()
    groups[2].start_swap()
    groups[3].start_swap()
    sent_all(back_args)

    left, right = pl.ds(0, HALF), pl.ds(HALF, HALF)
    for p in range(ROUNDS):
        for k, (a, b) in zip((1, 2, 3, 4, 5, 0), groups[p].finish()):
            out_proc[ROUNDS - 1 - p, k, :, left] = a
            out_proc[ROUNDS - 1 - p, k, :, right] = b
    for k, (a, b) in zip((1, 3, 2, 4, 5, 6), groups[2].finish()):
        out_enc[k, :, left] = a
        out_enc[k, :, right] = b
    last = groups[3].finish()
    out_enc[0, :, left], out_enc[0, :, right] = last[0]
    out_emb[...] = last[1][0][:, :variables]


def hand_over(*refs):
    count = len(refs) // 2
    for k in range(count):
        refs[count + k][...] = refs[k][...]


def on_device(
    cfg,
    grid_x,
    mesh_in,
    mesh_grad,
    embed_in,
    enc_weights,
    proc_weights,
    g2m_grid,
    g2m_mesh,
    mesh_send,
    mesh_recv,
    halo_idx,
):
    n = lax.axis_size("lon")
    count = g2m_grid.shape[0]
    cap = (count + n - 1) // n
    variables = grid_x.shape[1]
    mine = L // (cfg[0] * cfg[1] * cfg[2]) // 2
    plan = scratch_plan(cfg, n, n * cap, mesh_send.shape[0])
    vmem = pl.BlockSpec(memory_space=pltpu.VMEM)
    smem = pl.BlockSpec(memory_space=pltpu.SMEM)
    hbm = pl.BlockSpec(memory_space=pl.ANY)
    shapes = (
        jax.ShapeDtypeStruct((T, L), BF),
        jax.ShapeDtypeStruct((T, L), F32),
        jax.ShapeDtypeStruct((7, mine, L), F32),
        jax.ShapeDtypeStruct((ROUNDS, 6, mine, L), F32),
        jax.ShapeDtypeStruct((mine, variables), F32),
    )
    results = pl.pallas_call(
        functools.partial(kernel, cfg, n, cap, plan),
        out_shape=shapes,
        in_specs=[vmem] * 4 + [hbm] * 2 + [vmem] * 2 + [smem] * 3,
        out_specs=(vmem,) * 5,
        scratch_shapes=leaves(plan),
        compiler_params=pltpu.CompilerParams(
            collective_id=0, has_side_effects=True, vmem_limit_bytes=63 * 1024 * 1024
        ),
    )(
        grid_x.T,
        mesh_in,
        mesh_grad,
        embed_in,
        enc_weights,
        proc_weights,
        g2m_mesh.reshape(1, count),
        g2m_grid.reshape(1, count),
        mesh_send,
        mesh_recv,
        halo_idx.reshape(4),
    )
    latent, grad_in, enc, proc, emb_t = pl.pallas_call(
        hand_over,
        out_shape=shapes,
        in_specs=[vmem] * 5,
        out_specs=(vmem,) * 5,
    )(*results)
    return latent, grad_in, enc, proc, emb_t.T


def solution(mesh):
    n = mesh.shape["lon"]
    nx = 4 if n == 32 else 2
    cfg = (mesh.shape["lat"], n // (2 * nx), nx)
    return jax.shard_map(
        functools.partial(on_device, cfg),
        mesh=mesh,
        in_specs=(
            P(("lat", "lon"), None),
            P(("lat", "lon"), None),
            P(("lat", "lon"), None),
            P(),
            P(),
            P(),
            P(("lat", "lon")),
            P(("lat", "lon")),
            P(("lat", "lon")),
            P(("lat", "lon")),
            P(("lat", "lon"), None, None),
        ),
        out_specs=(
            P(("lat", "lon"), None),
            P(("lat", "lon"), None),
            P(None, ("lat", "lon"), None),
            P(None, None, ("lat", "lon"), None),
            P(None, ("lat", "lon")),
        ),
        check_vma=False,
    )
```

```python
import functools

import jax
import jax.numpy as jnp
from jax import lax
from jax.experimental import pallas as pl
from jax.experimental.pallas import tpu as pltpu
from jax.sharding import PartitionSpec as P

B = 32
L = 512
T = 256
MB = 8
ROUNDS = 2
EPSILON = 1e-05
BF = jnp.bfloat16
F32 = jnp.float32
MESH = pl.DeviceIdType.MESH
HALF = L // 2
OPPOSITE = (1, 0, 3, 2)
STRIDE = 19


def mm(a, b):
    return jnp.dot(a, b, preferred_element_type=F32)


def mt(a, b):
    return lax.dot_general(a, b, (((1,), (1,)), ((), ())), preferred_element_type=F32)


def tm(a, b):
    return lax.dot_general(a, b, (((0,), (0,)), ((), ())), preferred_element_type=F32)


def sigmoid(x):
    return 0.5 * jnp.tanh(0.5 * x) + 0.5


def swish(x):
    return x * sigmoid(x)


def swish_grad(x):
    s = sigmoid(x)
    return s * (1.0 + x * (1.0 - s))


def norm_rows(z):
    centred = z - jnp.mean(z, axis=-1, keepdims=True)
    r = lax.rsqrt(jnp.mean(centred * centred, axis=-1, keepdims=True) + EPSILON)
    return centred * r, r


def norm_back(g, y, r):
    return r * (
        g - jnp.mean(g, axis=-1, keepdims=True) - y * jnp.mean(g * y, axis=-1, keepdims=True)
    )


def iota(shape, dim):
    return lax.broadcasted_iota(jnp.int32, shape, dim)


def wide(r):
    return jnp.broadcast_to(r, (r.shape[0], 128))


class Group:
    def __init__(self, cfg, w, refs, sems, base, rows):
        self.cfg, self.w, self.refs, self.rows = cfg, w, refs, rows
        self.send, self.recv = sems
        self.base = base
        self.swapped = None
        self.lanes = []

    def copy(self, src, dst, index, device):
        c = pltpu.make_async_remote_copy(
            src_ref=src,
            dst_ref=dst,
            send_sem=self.send.at[index],
            recv_sem=self.recv.at[index],
            device_id=device,
            device_id_type=MESH,
        )
        c.start()
        return c

    def half(self, which):
        return pl.ds(pl.multiple_of(which * HALF, HALF), HALF)

    def start_core(self):
        w = self.w
        src = self.refs.own.at[:, :, :, :, self.half(1 - w.core)]
        self.core = self.copy(src, self.refs.crecv, self.base, (w.lat, w.sibling))

    def add_core(self):
        own, crecv = self.refs.own, self.refs.crecv
        mine = self.half(self.w.core)
        ny, nz, _ = self.cfg
        self.core.wait()

        def body(y, _):
            for z in range(nz):
                total = own[y, z, :, :, mine].astype(F32) + crecv[y, z].astype(F32)
                own[y, z, :, :, mine] = total.astype(BF)
            return 0

        lax.fori_loop(0, ny, body, 0)

    def step(self):
        for lane in self.lanes:
            lane.step()

    def start_swap(self):
        w = self.w
        self.step()
        self.swapped = self.copy(
            self.refs.fin, self.refs.swap, self.base + 1, (w.lat, w.sibling)
        )

    def finish(self):
        w, (ny, nz, nx) = self.w, self.cfg
        if self.swapped is not None:
            self.swapped.wait()
        per = L // (ny * nz * nx)
        mine, other = self.refs.fin[...], self.refs.swap[...]
        left = jnp.where(w.core == 0, mine, other)
        right = jnp.where(w.core == 0, other, mine)
        keep = []
        for k in range(self.rows // per):
            pair = []
            for side in (left, right):
                rows = side[k * per : (k + 1) * per]
                pair.append(jnp.where(w.core == 0, rows[: per // 2], rows[per // 2 :]))
            keep.append(pair)
        return keep


class Lane:
    def __init__(self, group, recvs, base, rows, cols, order):
        self.group, self.recvs, self.base = group, recvs, base
        self.rows, self.cols, self.order = rows, cols, order
        w = group.w
        self.at = (w.lat, w.z, w.x)
        self.fixed = [slice(None)] * 3
        self.stage = 0
        self.flying = []

    def index(self, fixed):
        start = pl.multiple_of(self.group.w.core * HALF + self.cols[0], 128)
        return tuple(fixed) + (pl.ds(*self.rows), pl.ds(start, self.cols[1]))

    def device(self, axis, to):
        y, z, x = [to if a == axis else c for a, c in enumerate(self.at)]
        return (y, (z * self.group.cfg[2] + x) * 2 + self.group.w.core)

    def step(self):
        if self.stage > 0:
            self.collect()
        if self.stage < len(self.order):
            self.launch()
        self.stage += 1

    def launch(self):
        axis, own = self.order[self.stage], self.group.refs.own
        size = self.group.cfg[axis]
        for j in range(1, size):
            to = lax.rem(self.at[axis] + j, size)
            there = list(self.fixed)
            there[axis] = to
            self.flying.append(
                self.group.copy(
                    own.at[self.index(there)],
                    self.recvs[self.stage].at[j - 1],
                    self.base,
                    self.device(axis, to),
                )
            )
            self.base += 1
        self.fixed[axis] = self.at[axis]

    def collect(self):
        own, recv = self.group.refs.own, self.recvs[self.stage - 1]
        for c in self.flying:
            c.wait()
        self.flying = []
        peers = recv.shape[0]
        free = [a for a in range(3) if isinstance(self.fixed[a], slice)]
        if not free:
            total = own[self.index(self.fixed)].astype(F32)
            for j in range(peers):
                total = total + recv[j].astype(F32)
            self.group.refs.fin[pl.ds(*self.rows), pl.ds(*self.cols)] = total
            return
        for i in range(self.group.cfg[free[0]]):
            here = list(self.fixed)
            here[free[0]] = i
            total = own[self.index(here)].astype(F32)
            for j in range(peers):
                total = total + recv[j, i].astype(F32)
            own[self.index(here)] = total.astype(BF)


class Space:
    pass


Y, Z, X = 0, 1, 2
GROUPS = (
    (6, ((0, 3, 0, HALF, (Y, Z, X)),)),
    (6, ((0, 3, 0, HALF, (Y, X, Z)),)),
    (6, ((0, 1, 0, HALF, (Y, Z, X)), (1, 1, 0, HALF, (Z, X, Y)), (2, 1, 0, HALF, (X, Y, Z)))),
    (2, ((0, 1, 0, HALF, (Y,)),)),
)


def scratch_plan(cfg, n, slots, edges):
    ny, nz, nx = cfg
    per = L // (ny * nz * nx)
    rows = slots * B
    ids = slots * 8
    v = Space()

    def vm(*shape, dtype=BF):
        return pltpu.VMEM(shape, dtype)

    v.encw = vm(7, L, L)
    v.procw = vm(ROUNDS, 6, L, L)
    v.gxp = vm(HALF, T)
    v.emb_pre = vm(T, L)
    v.emb_act = vm(T, L)
    v.grid_norm = vm(T, L)
    v.grid_r = vm(T, 128, dtype=F32)
    v.G = vm(rows, T)
    v.sendbuf = vm(rows, L)
    v.recvbuf = vm(rows, L)
    v.backbuf = vm(rows, L)
    v.ids_send = vm(ids, 128)
    v.ids_recv = vm(ids, 128)
    v.Pm = vm(rows, T)
    v.recv_proj = vm(T, L)
    v.g_pre = vm(rows, L)
    v.g_act = vm(rows, L)
    v.g_msg = vm(rows, L)
    v.g_r = vm(rows, 128)
    v.acc = vm(T, L, dtype=F32)
    v.gsum = vm(T, L)
    v.u_s, v.u_gate, v.u_hid, v.u_y, v.u_r = [], [], [], [], []
    for u in range(ROUNDS + 1):
        v.u_s.append(vm(T, L))
        v.u_gate.append(vm(T, L))
        v.u_hid.append(vm(T, L))
        v.u_y.append(vm(T, L))
        v.u_r.append(vm(T, 128, dtype=F32))
    v.dz = vm(T, L)
    v.dgate = vm(T, L)
    v.drecv = vm(T, L)
    v.Pc = vm(edges * B, 2 * T)
    v.Ph = vm(edges * B, 4 * B)
    v.H = vm(4 * B, T)
    v.lat, v.halo, v.hsend, v.bsend, v.brecv = [], [], [], [], []
    v.e_pre, v.e_act, v.e_msg, v.e_r = [], [], [], []
    for r in range(ROUNDS):
        v.lat.append(vm(T, L))
        v.halo.append(vm(4 * B, L))
        v.hsend.append(vm(4 * B, L))
        v.bsend.append(vm(4 * B, L))
        v.brecv.append(vm(4 * B, L))
        v.e_pre.append(vm(edges * B, L))
        v.e_act.append(vm(edges * B, L))
        v.e_msg.append(vm(edges * B, L))
        v.e_r.append(vm(edges * B, 128, dtype=F32))
    v.own, v.crecv, v.fin, v.swap, v.lanes = [], [], [], [], []
    sems = 0
    for p, (count, lanes) in enumerate(GROUPS):
        r = count * per
        v.own.append(vm(*cfg, r, L))
        if p < 2:
            v.crecv.append(vm(*cfg, r, HALF))
        v.fin.append(vm(r, HALF, dtype=F32))
        v.swap.append(vm(r, HALF, dtype=F32))
        sems += 2
        for _, some, _, width, order in lanes:
            left = [0, 1, 2]
            for axis in order:
                left.remove(axis)
                free = [cfg[a] for a in left]
                v.lanes.append(vm(cfg[axis] - 1, *free, some * 2 * per, width))
                sems += cfg[axis] - 1
    dma = pltpu.SemaphoreType.DMA
    v.direct = vm(n - 1, 2 * per, HALF)
    v.w_sem = dma((2,))
    v.direct_ss, v.direct_rs = dma((n,)), dma((n,))
    v.ids_ss, v.ids_rs = dma((n,)), dma((n,))
    v.fwd_ss, v.fwd_rs = dma((n,)), dma((n,))
    v.back_ss, v.back_rs = dma((n,)), dma((n,))
    v.halo_ss, v.halo_rs = dma((8 * ROUNDS,)), dma((8 * ROUNDS,))
    v.rs_ss, v.rs_rs = dma((sems,)), dma((sems,))
    return v


def leaves(plan):
    return [x for v in vars(plan).values() for x in (v if isinstance(v, list) else [v])]


def bind(plan, refs):
    rest, out = iter(refs), Space()
    for name, v in vars(plan).items():
        setattr(out, name, [next(rest) for _ in v] if isinstance(v, list) else next(rest))
    return out


def kernel(
    cfg,
    n,
    cap,
    plan,
    gxt,
    mesh_in,
    mgrad,
    emb,
    encw_hbm,
    procw_hbm,
    mrow,
    grow,
    msend,
    mrecv,
    hidx,
    out_lat,
    out_gin,
    out_enc,
    out_proc,
    out_emb,
    *scratch,
):
    s = bind(plan, scratch)
    ny, nz, nx = cfg
    per = L // (ny * nz * nx)
    slots = n * cap
    tiles = slots * B // T
    ppt = T // (cap * B)
    edges = msend.shape[0]
    variables = gxt.shape[0]

    w = Space()
    w.lat, w.lon = lax.axis_index("lat"), lax.axis_index("lon")
    w.core = lax.rem(w.lon, 2)
    w.sibling = w.lon + 1 - 2 * w.core
    w.x = lax.rem(w.lon // 2, nx)
    w.z = w.lon // (2 * nx)
    me = w.lon

    enc_copy = pltpu.make_async_copy(encw_hbm, s.encw, s.w_sem.at[0])
    proc_copy = pltpu.make_async_copy(procw_hbm, s.procw, s.w_sem.at[1])
    enc_copy.start()
    proc_copy.start()

    barrier = pltpu.get_barrier_semaphore()

    def greet(k, _):
        pl.semaphore_signal(
            barrier, inc=1, device_id=(w.lat, lax.rem(me + k, n)), device_id_type=MESH
        )
        return 0

    lax.fori_loop(1, n, greet, 0)
    for j in range(1, ny):
        pl.semaphore_signal(
            barrier, inc=1, device_id=(lax.rem(w.lat + j, ny), me), device_id_type=MESH
        )

    count = mrow.shape[1]
    owner = (mrow[...] >> 3) & (n - 1)
    owner_hot = jnp.where(iota((n, count), 0) == owner, 1.0, 0.0)
    same = tm(owner_hot.astype(BF), owner_hot.astype(BF))
    before = iota((count, count), 0) < iota((count, count), 1)
    rank = jnp.sum(jnp.where(before, same, 0.0), axis=0, keepdims=True)
    far_z = (owner // (2 * nx) + nz - w.z) & (nz - 1)
    far_x = ((owner // 2) & (nx - 1)) + nx - w.x & (nx - 1)
    far = (far_z * nx + far_x) * 2 + ((owner + w.core) & 1)
    place_of = (far * pow(STRIDE, -1, n) + n - 1) & (n - 1)
    slot = place_of.astype(F32) * cap + rank
    hot = iota((slots, count), 0).astype(F32) == slot
    block = jnp.sum(jnp.where(hot, grow[...].astype(F32) + 1.0, 0.0), axis=1, keepdims=True) - 1.0
    dest = (
        jnp.sum(jnp.where(hot, (mrow[...] & (MB - 1)).astype(F32) + 1.0, 0.0), axis=1, keepdims=True)
        - 1.0
    )
    spread = (iota((slots * 8, slots), 0) >> 3) == iota((slots * 8, slots), 1)
    s.ids_send[...] = mm(
        jnp.where(spread, 1.0, 0.0).astype(BF),
        jnp.broadcast_to(dest, (slots, 128)).astype(BF),
    ).astype(BF)

    def at_offset(p, sign):
        q = lax.rem(STRIDE * (p + 1), n)
        z = lax.rem(w.z + nz + sign * (q // (2 * nx)), nz)
        x = lax.rem(w.x + nx + sign * lax.rem(q // 2, nx), nx)
        return (z * nx + x) * 2 + lax.rem(w.core + lax.rem(q, 2), 2)

    def row_copy(src, dst, size, ss, rs, sign, p):
        at = pl.ds(pl.multiple_of(p * size, size), size)
        return pltpu.make_async_remote_copy(
            src_ref=src.at[at],
            dst_ref=dst.at[at],
            send_sem=ss.at[p],
            recv_sem=rs.at[p],
            device_id=(w.lat, at_offset(p, sign)),
            device_id_type=MESH,
        )

    ids_args = (s.ids_send, s.ids_recv, cap * 8, s.ids_ss, s.ids_rs, 1)
    fwd_args = (s.sendbuf, s.recvbuf, cap * B, s.fwd_ss, s.fwd_rs, 1)
    back_args = (s.sendbuf, s.backbuf, cap * B, s.back_ss, s.back_rs, -1)

    def sent_all(args):
        def body(p, _):
            row_copy(*args, p).wait_send()
            return 0

        lax.fori_loop(0, n - 1, body, 0)

    def keep_own(args):
        src, dst, size = args[:3]
        at = pl.ds((n - 1) * size, size)
        dst[at] = src[at]

    s.gxp[...] = jnp.zeros((HALF, T), BF)
    s.gxp[pl.ds(0, variables), :] = gxt[...]
    embp = s.sendbuf.at[pl.ds(0, HALF)]
    embp[...] = jnp.zeros((HALF, L), BF)
    embp[pl.ds(0, variables), :] = emb[...]
    emb_pre = tm(s.gxp[...], embp[...])
    s.emb_pre[...] = emb_pre.astype(BF)
    emb_act = swish(emb_pre).astype(BF)
    s.emb_act[...] = emb_act
    enc_copy.wait()
    encw = s.encw
    grid_norm, grid_r = norm_rows(mm(emb_act, encw[0]))
    s.grid_norm[...] = grid_norm.astype(BF)
    s.grid_r[...] = wide(grid_r)

    pl.semaphore_wait(barrier, n - 1 + ny - 1)
    col = iota((T, T), 1)
    diag = (col & (B - 1)) == (iota((T, T), 0) & (B - 1))
    col_block = (col >> 5).astype(F32)
    block_b = jnp.broadcast_to(block, (slots, T)).astype(BF)

    def fill(t, _):
        at = pl.ds(pl.multiple_of(t * T, T), T)
        expand = ((iota((T, slots), 0) + t * T) >> 5) == iota((T, slots), 1)
        value = mm(jnp.where(expand, 1.0, 0.0).astype(BF), block_b)
        pick = jnp.where(diag & (value == col_block), 1.0, 0.0).astype(BF)
        s.G[at] = pick
        s.sendbuf[at] = mm(pick, s.grid_norm[...]).astype(BF)
        for q in range(ppt):
            p = t * ppt + q

            @pl.when(p < n - 1)
            def _():
                row_copy(*ids_args, p).start()
                row_copy(*fwd_args, p).start()

        return 0

    lax.fori_loop(0, tiles, fill, 0)
    keep_own(ids_args)
    keep_own(fwd_args)

    s.recv_proj[...] = mm(mesh_in[...], encw[2]).astype(BF)
    out_gin[...] = mm(mesh_in[...], encw[4])

    def place(columns):
        col = iota((B, columns), 1)
        return (col & (B - 1)) == iota((B, columns), 0), col >> 5

    diag_c, block_c = place(2 * T)
    diag_h, block_h = place(4 * B)
    diag_l, block_l = place(T)
    for e in range(edges):
        sender = msend[e]
        local = jnp.where(sender < MB, sender, -1)
        hit = (block_c == local) | (block_c == mrecv[e] + MB)
        s.Pc[pl.ds(e * B, B)] = jnp.where(diag_c & hit, 1.0, 0.0).astype(BF)
        s.Ph[pl.ds(e * B, B)] = jnp.where(diag_h & (block_h == sender - MB), 1.0, 0.0).astype(BF)
    for k in range(4):
        s.H[pl.ds(k * B, B)] = jnp.where(diag_l & (block_l == hidx[k]), 1.0, 0.0).astype(BF)

    id_rows = ppt * cap * 8
    id_pick = iota((T, id_rows), 1) == ((iota((T, id_rows), 0) >> 5) << 3)
    id_pick = jnp.where(id_pick, 1.0, 0.0).astype(BF)

    def pick_mesh(t):
        value = mm(id_pick, s.ids_recv[pl.ds(pl.multiple_of(t * id_rows, id_rows), id_rows)])
        value = jnp.concatenate([value, value], axis=1)
        return jnp.where(diag & (value == col_block), 1.0, 0.0).astype(BF)

    s.acc[...] = jnp.zeros((T, L), F32)

    def edge_tile(t, _):
        for q in range(ppt):
            p = t * ppt + q

            @pl.when(p < n - 1)
            def _():
                row_copy(*ids_args, p).wait_recv()
                row_copy(*fwd_args, p).wait_recv()

        at = pl.ds(pl.multiple_of(t * T, T), T)
        pick = pick_mesh(t)
        s.Pm[at] = pick
        pre = mm(s.recvbuf[at], encw[1]) + mm(pick, s.recv_proj[...])
        s.g_pre[at] = pre.astype(BF)
        act = swish(pre).astype(BF)
        s.g_act[at] = act
        msg, r = norm_rows(mm(act, encw[3]))
        s.g_r[at] = wide(r).astype(BF)
        msg = msg.astype(BF)
        s.g_msg[at] = msg
        s.acc[...] += tm(pick, msg)
        return 0

    lax.fori_loop(0, tiles, edge_tile, 0)

    def update(u, h, early, total, wa, wo):
        sb = total.astype(BF)
        s.u_s[u][...] = sb
        gate = early + mm(sb, wa)
        s.u_gate[u][...] = gate.astype(BF)
        hid = swish(gate).astype(BF)
        s.u_hid[u][...] = hid
        y, r = norm_rows(mm(hid, wo))
        s.u_y[u][...] = y.astype(BF)
        s.u_r[u][...] = wide(r)
        return (h.astype(F32) + y).astype(BF)

    def update_back(u, wh, wa, wo):
        dz = norm_back(out_gin[...], s.u_y[u][...].astype(F32), s.u_r[u][:, :1]).astype(BF)
        s.dz[...] = dz
        dgate = (mt(dz, wo) * swish_grad(s.u_gate[u][...].astype(F32))).astype(BF)
        s.dgate[...] = dgate
        out_gin[...] += mt(dgate, wh)
        return mt(dgate, wa)

    def neighbour(k):
        if k < 2:
            return (lax.rem(w.lat + (ny - 1 if k == 0 else 1), ny), me)
        return (w.lat, lax.rem(me + (n - 1 if k == 2 else 1), n))

    def halo_copy(src, dst, event, k):
        j = OPPOSITE[k]
        return pltpu.make_async_remote_copy(
            src_ref=src.at[pl.ds(k * B, B)],
            dst_ref=dst.at[pl.ds(j * B, B)],
            send_sem=s.halo_ss.at[event * 4 + j],
            recv_sem=s.halo_rs.at[event * 4 + j],
            device_id=neighbour(k),
            device_id_type=MESH,
        )

    s.lat[0][...] = update(0, mesh_in[...], out_gin[...], s.acc[...], encw[5], encw[6])
    proc_copy.wait()
    procw = s.procw
    top, bottom = pl.ds(0, T), pl.ds(T, T)
    sent_all(ids_args)
    sent_all(fwd_args)
    proj = s.sendbuf.at[pl.ds(0, 2 * T)]
    mixed = s.sendbuf.at[pl.ds(4 * T, 2 * T)]

    for r in range(ROUNDS):
        latent = s.lat[r][...]
        s.hsend[r][...] = mm(s.H[...], latent).astype(BF)
        copies = [halo_copy(s.hsend[r], s.halo[r], r, k) for k in range(4)]
        for c in copies:
            c.start()
        proj[top] = mm(latent, procw[r, 0]).astype(BF)
        proj[bottom] = mm(latent, procw[r, 1]).astype(BF)
        mixed[...] = mm(s.Pc[...], proj[...]).astype(BF)
        out_gin[...] = mm(latent, procw[r, 3])
        for c in copies:
            c.wait()
        shown = mm(s.halo[r][...], procw[r, 0]).astype(BF)
        pre = mixed[...].astype(F32) + mm(s.Ph[...], shown)
        s.e_pre[r][...] = pre.astype(BF)
        act = swish(pre).astype(BF)
        s.e_act[r][...] = act
        msg, rstd = norm_rows(mm(act, procw[r, 2]))
        s.e_r[r][...] = wide(rstd)
        msg = msg.astype(BF)
        s.e_msg[r][...] = msg
        total = tm(s.Pc[:, bottom], msg)
        new = update(r + 1, latent, out_gin[...], total, procw[r, 4], procw[r, 5])
        if r + 1 < ROUNDS:
            s.lat[r + 1][...] = new
        else:
            out_lat[...] = new

    dproj_ref = s.sendbuf.at[pl.ds(2 * T, T)]
    groups = []
    sem = lane_at = 0
    for p, (count, lanes) in enumerate(GROUPS):
        refs = Space()
        refs.own, refs.fin, refs.swap = s.own[p], s.fin[p], s.swap[p]
        refs.crecv = s.crecv[p % 2].at[:, :, :, pl.ds(0, count * per), :]
        group = Group(cfg, w, refs, (s.rs_ss, s.rs_rs), sem, count * per)
        sem += 2
        for first, some, left, width, order in lanes:
            rows = (first * 2 * per, some * 2 * per)
            recvs = s.lanes[lane_at : lane_at + len(order)]
            group.lanes.append(Lane(group, recvs, sem, rows, (left, width), order))
            lane_at += len(order)
            sem += sum(cfg[axis] - 1 for axis in order)
        groups.append(group)

    def outer_pair(p, pair, first, second):
        band = L // ny
        for y in range(ny):
            at = pl.ds(y * band, band)
            both = [tm(a[:, at], b[...]).reshape(nz, nx, per, L) for a, b in (first, second)]
            rows = pl.ds(pair * 2 * per, 2 * per)
            s.own[p][y, :, :, rows, :] = jnp.concatenate(both, axis=2).astype(BF)

    out_gin[...] = mgrad[...].astype(F32)
    for r in reversed(range(ROUNDS)):
        p = ROUNDS - 1 - r
        gs = update_back(r + 1, procw[r, 3], procw[r, 4], procw[r, 5])
        gmsg = mm(s.Pc[:, bottom], gs.astype(BF))
        gz = norm_back(gmsg, s.e_msg[r][...].astype(F32), s.e_r[r][:, :1]).astype(BF)
        s.e_msg[r][...] = gz
        dpre = (mt(gz, procw[r, 2]) * swish_grad(s.e_pre[r][...].astype(F32))).astype(BF)
        s.e_pre[r][...] = dpre
        s.bsend[r][...] = tm(s.Ph[...], dpre).astype(BF)
        copies = [halo_copy(s.bsend[r], s.brecv[r], ROUNDS + r, k) for k in range(4)]
        for c in copies:
            c.start()
        mixed[...] = tm(s.Pc[...], s.e_pre[r][...]).astype(BF)
        drecv = mixed[bottom]
        s.drecv[...] = drecv
        out_gin[...] += mt(drecv, procw[r, 1])
        outer_pair(p, 0, (s.lat[r], s.drecv), (s.e_act[r], s.e_msg[r]))
        outer_pair(p, 1, (s.lat[r], s.dgate), (s.u_s[r + 1], s.dgate))
        if p > 0:
            groups[p - 1].add_core()
            groups[p - 1].step()
        for c in copies:
            c.wait()
        dproj = (mixed[top].astype(F32) + tm(s.H[...], s.brecv[r][...])).astype(BF)
        dproj_ref[...] = dproj
        out_gin[...] += mt(dproj, procw[r, 0])
        outer_pair(p, 2, (s.u_hid[r + 1], s.dz), (s.lat[r], dproj_ref))
        groups[p].start_core()

    gs = update_back(0, encw[4], encw[5], encw[6])
    s.gsum[...] = gs.astype(BF)
    s.acc[...] = jnp.zeros((T, L), F32)

    def edge_back(t, _):
        at = pl.ds(pl.multiple_of(t * T, T), T)
        pick = s.Pm[at]
        gmsg = mm(pick, s.gsum[...])
        gz = norm_back(gmsg, s.g_msg[at].astype(F32), s.g_r[at, :1].astype(F32)).astype(BF)
        s.g_msg[at] = gz
        dpre = (mt(gz, encw[3]) * swish_grad(s.g_pre[at].astype(F32))).astype(BF)
        s.g_pre[at] = dpre
        s.acc[...] += tm(pick, dpre)
        s.sendbuf[at] = mt(dpre, encw[1]).astype(BF)
        for q in range(ppt):
            p = t * ppt + q

            @pl.when(p < n - 1)
            def _():
                row_copy(*back_args, p).start()

        return 0

    lax.fori_loop(0, tiles // 2, edge_back, 0)
    groups[1].add_core()
    groups[1].step()
    lax.fori_loop(tiles // 2, tiles, edge_back, 0)
    keep_own(back_args)
    drecv = s.acc[...].astype(BF)
    s.drecv[...] = drecv
    out_gin[...] += mt(drecv, encw[2])
    outer_pair(2, 0, (s.recvbuf, s.g_pre), (s.g_act, s.g_msg))
    outer_pair(2, 1, (mesh_in, s.drecv), (mesh_in, s.dgate))
    outer_pair(2, 2, (s.u_s[0], s.dgate), (s.u_hid[0], s.dz))
    groups[2].start_core()

    s.acc[...] = jnp.zeros((T, L), F32)

    def back_tile(t, _):
        for q in range(ppt):
            p = t * ppt + q

            @pl.when(p < n - 1)
            def _():
                row_copy(*back_args, p).wait_recv()

        at = pl.ds(pl.multiple_of(t * T, T), T)
        s.acc[...] += tm(s.G[at], s.backbuf[at])
        return 0

    lax.fori_loop(0, tiles, back_tile, 0)
    groups[0].step()
    groups[2].add_core()
    groups[2].step()
    dgz = norm_back(s.acc[...], s.grid_norm[...].astype(F32), s.grid_r[:, :1]).astype(BF)
    dgpre = (mt(dgz, encw[0]) * swish_grad(s.emb_pre[...].astype(F32))).astype(BF)
    first = tm(s.emb_act[...], dgz).reshape(ny, nz, nx, per, L)
    second = mm(s.gxp[...], dgpre).T.reshape(ny, nz, nx, per, HALF)
    second = jnp.concatenate([second, jnp.zeros_like(second)], axis=4)
    s.own[3][...] = jnp.concatenate([first, second], axis=3).astype(BF)
    groups[3].start_core()

    def direct_copy(p):
        to = at_offset(p, 1)
        mine = groups[3].half(w.core)
        return pltpu.make_async_remote_copy(
            src_ref=s.own[3].at[w.lat, to // (2 * nx), lax.rem(to // 2, nx), :, mine],
            dst_ref=s.direct.at[p],
            send_sem=s.direct_ss.at[p],
            recv_sem=s.direct_rs.at[p],
            device_id=(w.lat, to),
            device_id_type=MESH,
        )

    def direct_start(p, _):
        direct_copy(p).start()
        return 0

    def direct_wait(p, _):
        direct_copy(p).wait()
        return 0

    groups[3].add_core()
    groups[3].step()
    groups[1].step()
    groups[0].step()
    groups[2].step()
    groups[3].step()
    lax.fori_loop(0, n - 1, direct_start, 0)
    groups[1].step()
    groups[0].start_swap()
    groups[2].step()
    groups[1].start_swap()
    groups[2].start_swap()
    lax.fori_loop(0, n - 1, direct_wait, 0)
    same = s.own[3][w.lat, w.z, w.x, :, groups[3].half(w.core)].astype(F32)
    other = jnp.zeros((2 * per, HALF), F32)
    for p in range(n - 1):
        if STRIDE * (p + 1) % n % 2 == 0:
            same = same + s.direct[p].astype(F32)
        else:
            other = other + s.direct[p].astype(F32)
    s.fin[3][...] = same
    s.swap[3][...] = other
    sent_all(back_args)

    left, right = pl.ds(0, HALF), pl.ds(HALF, HALF)
    for p in range(ROUNDS):
        for k, (a, b) in zip((1, 2, 3, 4, 5, 0), groups[p].finish()):
            out_proc[ROUNDS - 1 - p, k, :, left] = a
            out_proc[ROUNDS - 1 - p, k, :, right] = b
    for k, (a, b) in zip((1, 3, 2, 4, 5, 6), groups[2].finish()):
        out_enc[k, :, left] = a
        out_enc[k, :, right] = b
    last = groups[3].finish()
    out_enc[0, :, left], out_enc[0, :, right] = last[0]
    out_emb[...] = last[1][0][:, :variables]


def hand_over(*refs):
    count = len(refs) // 2
    for k in range(count):
        refs[count + k][...] = refs[k][...]


def on_device(
    cfg,
    grid_x,
    mesh_in,
    mesh_grad,
    embed_in,
    enc_weights,
    proc_weights,
    g2m_grid,
    g2m_mesh,
    mesh_send,
    mesh_recv,
    halo_idx,
):
    n = lax.axis_size("lon")
    count = g2m_grid.shape[0]
    cap = (count + n - 1) // n
    variables = grid_x.shape[1]
    mine = L // (cfg[0] * cfg[1] * cfg[2]) // 2
    plan = scratch_plan(cfg, n, n * cap, mesh_send.shape[0])
    vmem = pl.BlockSpec(memory_space=pltpu.VMEM)
    smem = pl.BlockSpec(memory_space=pltpu.SMEM)
    hbm = pl.BlockSpec(memory_space=pl.ANY)
    shapes = (
        jax.ShapeDtypeStruct((T, L), BF),
        jax.ShapeDtypeStruct((T, L), F32),
        jax.ShapeDtypeStruct((7, mine, L), F32),
        jax.ShapeDtypeStruct((ROUNDS, 6, mine, L), F32),
        jax.ShapeDtypeStruct((mine, variables), F32),
    )
    results = pl.pallas_call(
        functools.partial(kernel, cfg, n, cap, plan),
        out_shape=shapes,
        in_specs=[vmem] * 4 + [hbm] * 2 + [vmem] * 2 + [smem] * 3,
        out_specs=(vmem,) * 5,
        scratch_shapes=leaves(plan),
        compiler_params=pltpu.CompilerParams(
            collective_id=0, has_side_effects=True, vmem_limit_bytes=63 * 1024 * 1024
        ),
    )(
        grid_x.T,
        mesh_in,
        mesh_grad,
        embed_in,
        enc_weights,
        proc_weights,
        g2m_mesh.reshape(1, count),
        g2m_grid.reshape(1, count),
        mesh_send,
        mesh_recv,
        halo_idx.reshape(4),
    )
    latent, grad_in, enc, proc, emb_t = pl.pallas_call(
        hand_over,
        out_shape=shapes,
        in_specs=[vmem] * 5,
        out_specs=(vmem,) * 5,
    )(*results)
    return latent, grad_in, enc, proc, emb_t.T


def solution(mesh):
    n = mesh.shape["lon"]
    nx = 4 if n == 32 else 2
    cfg = (mesh.shape["lat"], n // (2 * nx), nx)
    return jax.shard_map(
        functools.partial(on_device, cfg),
        mesh=mesh,
        in_specs=(
            P(("lat", "lon"), None),
            P(("lat", "lon"), None),
            P(("lat", "lon"), None),
            P(),
            P(),
            P(),
            P(("lat", "lon")),
            P(("lat", "lon")),
            P(("lat", "lon")),
            P(("lat", "lon")),
            P(("lat", "lon"), None, None),
        ),
        out_specs=(
            P(("lat", "lon"), None),
            P(("lat", "lon"), None),
            P(None, ("lat", "lon"), None),
            P(None, None, ("lat", "lon"), None),
            P(None, ("lat", "lon")),
        ),
        check_vma=False,
    )
```

```python
import functools

import jax
import jax.numpy as jnp
from jax import lax
from jax.experimental import pallas as pl
from jax.experimental.pallas import tpu as pltpu
from jax.sharding import PartitionSpec as P

B = 32
L = 512
T = 256
MB = 8
ROUNDS = 2
EPSILON = 1e-05
BF = jnp.bfloat16
F32 = jnp.float32
MESH = pl.DeviceIdType.MESH
HALF = L // 2
OPPOSITE = (1, 0, 3, 2)
STRIDE = 13


def mm(a, b):
    return jnp.dot(a, b, preferred_element_type=F32)


def mt(a, b):
    return lax.dot_general(a, b, (((1,), (1,)), ((), ())), preferred_element_type=F32)


def tm(a, b):
    return lax.dot_general(a, b, (((0,), (0,)), ((), ())), preferred_element_type=F32)


def sigmoid(x):
    return 0.5 * jnp.tanh(0.5 * x) + 0.5


def swish(x):
    return x * sigmoid(x)


def swish_grad(x):
    s = sigmoid(x)
    return s * (1.0 + x * (1.0 - s))


def norm_rows(z):
    centred = z - jnp.mean(z, axis=-1, keepdims=True)
    r = lax.rsqrt(jnp.mean(centred * centred, axis=-1, keepdims=True) + EPSILON)
    return centred * r, r


def norm_back(g, y, r):
    return r * (
        g - jnp.mean(g, axis=-1, keepdims=True) - y * jnp.mean(g * y, axis=-1, keepdims=True)
    )


def iota(shape, dim):
    return lax.broadcasted_iota(jnp.int32, shape, dim)


def wide(r):
    return jnp.broadcast_to(r, (r.shape[0], 128))


class Group:
    def __init__(self, cfg, w, refs, sems, base, rows):
        self.cfg, self.w, self.refs, self.rows = cfg, w, refs, rows
        self.send, self.recv = sems
        self.base = base
        self.swapped = None
        self.lanes = []

    def copy(self, src, dst, index, device):
        c = pltpu.make_async_remote_copy(
            src_ref=src,
            dst_ref=dst,
            send_sem=self.send.at[index],
            recv_sem=self.recv.at[index],
            device_id=device,
            device_id_type=MESH,
        )
        c.start()
        return c

    def half(self, which):
        return pl.ds(pl.multiple_of(which * HALF, HALF), HALF)

    def start_core(self):
        w = self.w
        src = self.refs.own.at[:, :, :, :, self.half(1 - w.core)]
        self.core = self.copy(src, self.refs.crecv, self.base, (w.lat, w.sibling))

    def add_core(self):
        own, crecv = self.refs.own, self.refs.crecv
        mine = self.half(self.w.core)
        ny, nz, _ = self.cfg
        self.core.wait()

        def body(y, _):
            for z in range(nz):
                total = own[y, z, :, :, mine].astype(F32) + crecv[y, z].astype(F32)
                own[y, z, :, :, mine] = total.astype(BF)
            return 0

        lax.fori_loop(0, ny, body, 0)

    def step(self):
        for lane in self.lanes:
            lane.step()

    def start_swap(self):
        w = self.w
        self.step()
        self.swapped = self.copy(
            self.refs.fin, self.refs.swap, self.base + 1, (w.lat, w.sibling)
        )

    def finish(self):
        w, (ny, nz, nx) = self.w, self.cfg
        if self.swapped is not None:
            self.swapped.wait()
        per = L // (ny * nz * nx)
        mine, other = self.refs.fin[...], self.refs.swap[...]
        left = jnp.where(w.core == 0, mine, other)
        right = jnp.where(w.core == 0, other, mine)
        keep = []
        for k in range(self.rows // per):
            pair = []
            for side in (left, right):
                rows = side[k * per : (k + 1) * per]
                pair.append(jnp.where(w.core == 0, rows[: per // 2], rows[per // 2 :]))
            keep.append(pair)
        return keep


class Lane:
    def __init__(self, group, recvs, base, rows, cols, order):
        self.group, self.recvs, self.base = group, recvs, base
        self.rows, self.cols, self.order = rows, cols, order
        w = group.w
        self.at = (w.lat, w.z, w.x)
        self.fixed = [slice(None)] * 3
        self.stage = 0
        self.flying = []

    def index(self, fixed):
        start = pl.multiple_of(self.group.w.core * HALF + self.cols[0], 128)
        return tuple(fixed) + (pl.ds(*self.rows), pl.ds(start, self.cols[1]))

    def device(self, axis, to):
        y, z, x = [to if a == axis else c for a, c in enumerate(self.at)]
        return (y, (z * self.group.cfg[2] + x) * 2 + self.group.w.core)

    def step(self):
        if self.stage > 0:
            self.collect()
        if self.stage < len(self.order):
            self.launch()
        self.stage += 1

    def launch(self):
        axis, own = self.order[self.stage], self.group.refs.own
        size = self.group.cfg[axis]
        for j in range(1, size):
            to = lax.rem(self.at[axis] + j, size)
            there = list(self.fixed)
            there[axis] = to
            self.flying.append(
                self.group.copy(
                    own.at[self.index(there)],
                    self.recvs[self.stage].at[j - 1],
                    self.base,
                    self.device(axis, to),
                )
            )
            self.base += 1
        self.fixed[axis] = self.at[axis]

    def collect(self):
        own, recv = self.group.refs.own, self.recvs[self.stage - 1]
        for c in self.flying:
            c.wait()
        self.flying = []
        peers = recv.shape[0]
        free = [a for a in range(3) if isinstance(self.fixed[a], slice)]
        if not free:
            total = own[self.index(self.fixed)].astype(F32)
            for j in range(peers):
                total = total + recv[j].astype(F32)
            self.group.refs.fin[pl.ds(*self.rows), pl.ds(*self.cols)] = total
            return
        for i in range(self.group.cfg[free[0]]):
            here = list(self.fixed)
            here[free[0]] = i
            total = own[self.index(here)].astype(F32)
            for j in range(peers):
                total = total + recv[j, i].astype(F32)
            own[self.index(here)] = total.astype(BF)


class Space:
    pass


Y, Z, X = 0, 1, 2
GROUPS = (
    (6, ((0, 3, 0, HALF, (Y, Z, X)),)),
    (6, ((0, 3, 0, HALF, (Y, X, Z)),)),
    (6, ((0, 1, 0, HALF, (Y, Z, X)), (1, 1, 0, HALF, (Z, X, Y)), (2, 1, 0, HALF, (X, Y, Z)))),
    (2, ((0, 1, 0, HALF, (Y,)),)),
)


def scratch_plan(cfg, n, slots, edges):
    ny, nz, nx = cfg
    per = L // (ny * nz * nx)
    rows = slots * B
    ids = slots * 8
    v = Space()

    def vm(*shape, dtype=BF):
        return pltpu.VMEM(shape, dtype)

    v.encw = vm(7, L, L)
    v.procw = vm(ROUNDS, 6, L, L)
    v.gxp = vm(HALF, T)
    v.emb_pre = vm(T, L)
    v.emb_act = vm(T, L)
    v.grid_norm = vm(T, L)
    v.grid_r = vm(T, 128, dtype=F32)
    v.G = vm(rows, T)
    v.sendbuf = vm(rows, L)
    v.recvbuf = vm(rows, L)
    v.backbuf = vm(rows, L)
    v.ids_send = vm(ids, 128)
    v.ids_recv = vm(ids, 128)
    v.Pm = vm(rows, T)
    v.recv_proj = vm(T, L)
    v.g_pre = vm(rows, L)
    v.g_act = vm(rows, L)
    v.g_msg = vm(rows, L)
    v.g_r = vm(rows, 128)
    v.acc = vm(T, L, dtype=F32)
    v.gsum = vm(T, L)
    v.u_s, v.u_gate, v.u_hid, v.u_y, v.u_r = [], [], [], [], []
    for u in range(ROUNDS + 1):
        v.u_s.append(vm(T, L))
        v.u_gate.append(vm(T, L))
        v.u_hid.append(vm(T, L))
        v.u_y.append(vm(T, L))
        v.u_r.append(vm(T, 128, dtype=F32))
    v.dz = vm(T, L)
    v.dgate = vm(T, L)
    v.drecv = vm(T, L)
    v.Pc = vm(edges * B, 2 * T)
    v.Ph = vm(edges * B, 4 * B)
    v.H = vm(4 * B, T)
    v.lat, v.halo, v.hsend, v.bsend, v.brecv = [], [], [], [], []
    v.e_pre, v.e_act, v.e_msg, v.e_r = [], [], [], []
    for r in range(ROUNDS):
        v.lat.append(vm(T, L))
        v.halo.append(vm(4 * B, L))
        v.hsend.append(vm(4 * B, L))
        v.bsend.append(vm(4 * B, L))
        v.brecv.append(vm(4 * B, L))
        v.e_pre.append(vm(edges * B, L))
        v.e_act.append(vm(edges * B, L))
        v.e_msg.append(vm(edges * B, L))
        v.e_r.append(vm(edges * B, 128, dtype=F32))
    v.own, v.crecv, v.fin, v.swap, v.lanes = [], [], [], [], []
    sems = 0
    for p, (count, lanes) in enumerate(GROUPS):
        r = count * per
        v.own.append(vm(*cfg, r, L))
        if p < 2:
            v.crecv.append(vm(*cfg, r, HALF))
        v.fin.append(vm(r, HALF, dtype=F32))
        v.swap.append(vm(r, HALF, dtype=F32))
        sems += 2
        for _, some, _, width, order in lanes:
            left = [0, 1, 2]
            for axis in order:
                left.remove(axis)
                free = [cfg[a] for a in left]
                v.lanes.append(vm(cfg[axis] - 1, *free, some * 2 * per, width))
                sems += cfg[axis] - 1
    dma = pltpu.SemaphoreType.DMA
    v.direct = vm(n - 1, 2 * per, HALF)
    v.w_sem = dma((2,))
    v.direct_ss, v.direct_rs = dma((n,)), dma((n,))
    v.ids_ss, v.ids_rs = dma((n,)), dma((n,))
    v.fwd_ss, v.fwd_rs = dma((n,)), dma((n,))
    v.back_ss, v.back_rs = dma((n,)), dma((n,))
    v.halo_ss, v.halo_rs = dma((8 * ROUNDS,)), dma((8 * ROUNDS,))
    v.rs_ss, v.rs_rs = dma((sems,)), dma((sems,))
    return v


def leaves(plan):
    return [x for v in vars(plan).values() for x in (v if isinstance(v, list) else [v])]


def bind(plan, refs):
    rest, out = iter(refs), Space()
    for name, v in vars(plan).items():
        setattr(out, name, [next(rest) for _ in v] if isinstance(v, list) else next(rest))
    return out


def kernel(
    cfg,
    n,
    cap,
    plan,
    gxt,
    mesh_in,
    mgrad,
    emb,
    encw_hbm,
    procw_hbm,
    mrow,
    grow,
    msend,
    mrecv,
    hidx,
    out_lat,
    out_gin,
    out_enc,
    out_proc,
    out_emb,
    *scratch,
):
    s = bind(plan, scratch)
    ny, nz, nx = cfg
    per = L // (ny * nz * nx)
    slots = n * cap
    tiles = slots * B // T
    ppt = T // (cap * B)
    edges = msend.shape[0]
    variables = gxt.shape[0]

    w = Space()
    w.lat, w.lon = lax.axis_index("lat"), lax.axis_index("lon")
    w.core = lax.rem(w.lon, 2)
    w.sibling = w.lon + 1 - 2 * w.core
    w.x = lax.rem(w.lon // 2, nx)
    w.z = w.lon // (2 * nx)
    me = w.lon

    enc_copy = pltpu.make_async_copy(encw_hbm, s.encw, s.w_sem.at[0])
    proc_copy = pltpu.make_async_copy(procw_hbm, s.procw, s.w_sem.at[1])
    enc_copy.start()
    proc_copy.start()

    barrier = pltpu.get_barrier_semaphore()

    def greet(k, _):
        pl.semaphore_signal(
            barrier, inc=1, device_id=(w.lat, lax.rem(me + k, n)), device_id_type=MESH
        )
        return 0

    lax.fori_loop(1, n, greet, 0)
    for j in range(1, ny):
        pl.semaphore_signal(
            barrier, inc=1, device_id=(lax.rem(w.lat + j, ny), me), device_id_type=MESH
        )

    count = mrow.shape[1]
    owner = (mrow[...] >> 3) & (n - 1)
    owner_hot = jnp.where(iota((n, count), 0) == owner, 1.0, 0.0)
    same = tm(owner_hot.astype(BF), owner_hot.astype(BF))
    before = iota((count, count), 0) < iota((count, count), 1)
    rank = jnp.sum(jnp.where(before, same, 0.0), axis=0, keepdims=True)
    far_z = (owner // (2 * nx) + nz - w.z) & (nz - 1)
    far_x = ((owner // 2) & (nx - 1)) + nx - w.x & (nx - 1)
    far = (far_z * nx + far_x) * 2 + ((owner + w.core) & 1)
    place_of = (far * pow(STRIDE, -1, n) + n - 1) & (n - 1)
    slot = place_of.astype(F32) * cap + rank
    hot = iota((slots, count), 0).astype(F32) == slot
    block = jnp.sum(jnp.where(hot, grow[...].astype(F32) + 1.0, 0.0), axis=1, keepdims=True) - 1.0
    dest = (
        jnp.sum(jnp.where(hot, (mrow[...] & (MB - 1)).astype(F32) + 1.0, 0.0), axis=1, keepdims=True)
        - 1.0
    )
    spread = (iota((slots * 8, slots), 0) >> 3) == iota((slots * 8, slots), 1)
    s.ids_send[...] = mm(
        jnp.where(spread, 1.0, 0.0).astype(BF),
        jnp.broadcast_to(dest, (slots, 128)).astype(BF),
    ).astype(BF)

    def at_offset(p, sign):
        q = lax.rem(STRIDE * (p + 1), n)
        z = lax.rem(w.z + nz + sign * (q // (2 * nx)), nz)
        x = lax.rem(w.x + nx + sign * lax.rem(q // 2, nx), nx)
        return (z * nx + x) * 2 + lax.rem(w.core + lax.rem(q, 2), 2)

    def row_copy(src, dst, size, ss, rs, sign, p):
        at = pl.ds(pl.multiple_of(p * size, size), size)
        return pltpu.make_async_remote_copy(
            src_ref=src.at[at],
            dst_ref=dst.at[at],
            send_sem=ss.at[p],
            recv_sem=rs.at[p],
            device_id=(w.lat, at_offset(p, sign)),
            device_id_type=MESH,
        )

    ids_args = (s.ids_send, s.ids_recv, cap * 8, s.ids_ss, s.ids_rs, 1)
    fwd_args = (s.sendbuf, s.recvbuf, cap * B, s.fwd_ss, s.fwd_rs, 1)
    back_args = (s.sendbuf, s.backbuf, cap * B, s.back_ss, s.back_rs, -1)

    def sent_all(args):
        def body(p, _):
            row_copy(*args, p).wait_send()
            return 0

        lax.fori_loop(0, n - 1, body, 0)

    def keep_own(args):
        src, dst, size = args[:3]
        at = pl.ds((n - 1) * size, size)
        dst[at] = src[at]

    s.gxp[...] = jnp.zeros((HALF, T), BF)
    s.gxp[pl.ds(0, variables), :] = gxt[...]
    embp = s.sendbuf.at[pl.ds(0, HALF)]
    embp[...] = jnp.zeros((HALF, L), BF)
    embp[pl.ds(0, variables), :] = emb[...]
    emb_pre = tm(s.gxp[...], embp[...])
    s.emb_pre[...] = emb_pre.astype(BF)
    emb_act = swish(emb_pre).astype(BF)
    s.emb_act[...] = emb_act
    enc_copy.wait()
    encw = s.encw
    grid_norm, grid_r = norm_rows(mm(emb_act, encw[0]))
    s.grid_norm[...] = grid_norm.astype(BF)
    s.grid_r[...] = wide(grid_r)

    pl.semaphore_wait(barrier, n - 1 + ny - 1)
    col = iota((T, T), 1)
    diag = (col & (B - 1)) == (iota((T, T), 0) & (B - 1))
    col_block = (col >> 5).astype(F32)
    block_b = jnp.broadcast_to(block, (slots, T)).astype(BF)

    def fill(t, _):
        at = pl.ds(pl.multiple_of(t * T, T), T)
        expand = ((iota((T, slots), 0) + t * T) >> 5) == iota((T, slots), 1)
        value = mm(jnp.where(expand, 1.0, 0.0).astype(BF), block_b)
        pick = jnp.where(diag & (value == col_block), 1.0, 0.0).astype(BF)
        s.G[at] = pick
        s.sendbuf[at] = mm(pick, s.grid_norm[...]).astype(BF)
        for q in range(ppt):
            p = t * ppt + q

            @pl.when(p < n - 1)
            def _():
                row_copy(*ids_args, p).start()
                row_copy(*fwd_args, p).start()

        return 0

    lax.fori_loop(0, tiles, fill, 0)
    keep_own(ids_args)
    keep_own(fwd_args)

    s.recv_proj[...] = mm(mesh_in[...], encw[2]).astype(BF)
    out_gin[...] = mm(mesh_in[...], encw[4])

    def place(columns):
        col = iota((B, columns), 1)
        return (col & (B - 1)) == iota((B, columns), 0), col >> 5

    diag_c, block_c = place(2 * T)
    diag_h, block_h = place(4 * B)
    diag_l, block_l = place(T)
    for e in range(edges):
        sender = msend[e]
        local = jnp.where(sender < MB, sender, -1)
        hit = (block_c == local) | (block_c == mrecv[e] + MB)
        s.Pc[pl.ds(e * B, B)] = jnp.where(diag_c & hit, 1.0, 0.0).astype(BF)
        s.Ph[pl.ds(e * B, B)] = jnp.where(diag_h & (block_h == sender - MB), 1.0, 0.0).astype(BF)
    for k in range(4):
        s.H[pl.ds(k * B, B)] = jnp.where(diag_l & (block_l == hidx[k]), 1.0, 0.0).astype(BF)

    id_rows = ppt * cap * 8
    id_pick = iota((T, id_rows), 1) == ((iota((T, id_rows), 0) >> 5) << 3)
    id_pick = jnp.where(id_pick, 1.0, 0.0).astype(BF)

    def pick_mesh(t):
        value = mm(id_pick, s.ids_recv[pl.ds(pl.multiple_of(t * id_rows, id_rows), id_rows)])
        value = jnp.concatenate([value, value], axis=1)
        return jnp.where(diag & (value == col_block), 1.0, 0.0).astype(BF)

    s.acc[...] = jnp.zeros((T, L), F32)

    def edge_tile(t, _):
        for q in range(ppt):
            p = t * ppt + q

            @pl.when(p < n - 1)
            def _():
                row_copy(*ids_args, p).wait_recv()
                row_copy(*fwd_args, p).wait_recv()

        at = pl.ds(pl.multiple_of(t * T, T), T)
        pick = pick_mesh(t)
        s.Pm[at] = pick
        pre = mm(s.recvbuf[at], encw[1]) + mm(pick, s.recv_proj[...])
        s.g_pre[at] = pre.astype(BF)
        act = swish(pre).astype(BF)
        s.g_act[at] = act
        msg, r = norm_rows(mm(act, encw[3]))
        s.g_r[at] = wide(r).astype(BF)
        msg = msg.astype(BF)
        s.g_msg[at] = msg
        s.acc[...] += tm(pick, msg)
        return 0

    lax.fori_loop(0, tiles, edge_tile, 0)

    def update(u, h, early, total, wa, wo):
        sb = total.astype(BF)
        s.u_s[u][...] = sb
        gate = early + mm(sb, wa)
        s.u_gate[u][...] = gate.astype(BF)
        hid = swish(gate).astype(BF)
        s.u_hid[u][...] = hid
        y, r = norm_rows(mm(hid, wo))
        s.u_y[u][...] = y.astype(BF)
        s.u_r[u][...] = wide(r)
        return (h.astype(F32) + y).astype(BF)

    def update_back(u, wh, wa, wo):
        dz = norm_back(out_gin[...], s.u_y[u][...].astype(F32), s.u_r[u][:, :1]).astype(BF)
        s.dz[...] = dz
        dgate = (mt(dz, wo) * swish_grad(s.u_gate[u][...].astype(F32))).astype(BF)
        s.dgate[...] = dgate
        out_gin[...] += mt(dgate, wh)
        return mt(dgate, wa)

    def neighbour(k):
        if k < 2:
            return (lax.rem(w.lat + (ny - 1 if k == 0 else 1), ny), me)
        return (w.lat, lax.rem(me + (n - 1 if k == 2 else 1), n))

    def halo_copy(src, dst, event, k):
        j = OPPOSITE[k]
        return pltpu.make_async_remote_copy(
            src_ref=src.at[pl.ds(k * B, B)],
            dst_ref=dst.at[pl.ds(j * B, B)],
            send_sem=s.halo_ss.at[event * 4 + j],
            recv_sem=s.halo_rs.at[event * 4 + j],
            device_id=neighbour(k),
            device_id_type=MESH,
        )

    s.lat[0][...] = update(0, mesh_in[...], out_gin[...], s.acc[...], encw[5], encw[6])
    proc_copy.wait()
    procw = s.procw
    top, bottom = pl.ds(0, T), pl.ds(T, T)
    sent_all(ids_args)
    sent_all(fwd_args)
    proj = s.sendbuf.at[pl.ds(0, 2 * T)]
    mixed = s.sendbuf.at[pl.ds(4 * T, 2 * T)]

    for r in range(ROUNDS):
        latent = s.lat[r][...]
        s.hsend[r][...] = mm(s.H[...], latent).astype(BF)
        copies = [halo_copy(s.hsend[r], s.halo[r], r, k) for k in range(4)]
        for c in copies:
            c.start()
        proj[top] = mm(latent, procw[r, 0]).astype(BF)
        proj[bottom] = mm(latent, procw[r, 1]).astype(BF)
        mixed[...] = mm(s.Pc[...], proj[...]).astype(BF)
        out_gin[...] = mm(latent, procw[r, 3])
        for c in copies:
            c.wait()
        shown = mm(s.halo[r][...], procw[r, 0]).astype(BF)
        pre = mixed[...].astype(F32) + mm(s.Ph[...], shown)
        s.e_pre[r][...] = pre.astype(BF)
        act = swish(pre).astype(BF)
        s.e_act[r][...] = act
        msg, rstd = norm_rows(mm(act, procw[r, 2]))
        s.e_r[r][...] = wide(rstd)
        msg = msg.astype(BF)
        s.e_msg[r][...] = msg
        total = tm(s.Pc[:, bottom], msg)
        new = update(r + 1, latent, out_gin[...], total, procw[r, 4], procw[r, 5])
        if r + 1 < ROUNDS:
            s.lat[r + 1][...] = new
        else:
            out_lat[...] = new

    dproj_ref = s.sendbuf.at[pl.ds(2 * T, T)]
    groups = []
    sem = lane_at = 0
    for p, (count, lanes) in enumerate(GROUPS):
        refs = Space()
        refs.own, refs.fin, refs.swap = s.own[p], s.fin[p], s.swap[p]
        refs.crecv = s.crecv[p % 2].at[:, :, :, pl.ds(0, count * per), :]
        group = Group(cfg, w, refs, (s.rs_ss, s.rs_rs), sem, count * per)
        sem += 2
        for first, some, left, width, order in lanes:
            rows = (first * 2 * per, some * 2 * per)
            recvs = s.lanes[lane_at : lane_at + len(order)]
            group.lanes.append(Lane(group, recvs, sem, rows, (left, width), order))
            lane_at += len(order)
            sem += sum(cfg[axis] - 1 for axis in order)
        groups.append(group)

    def outer_pair(p, pair, first, second):
        band = L // ny
        for y in range(ny):
            at = pl.ds(y * band, band)
            both = [tm(a[:, at], b[...]).reshape(nz, nx, per, L) for a, b in (first, second)]
            rows = pl.ds(pair * 2 * per, 2 * per)
            s.own[p][y, :, :, rows, :] = jnp.concatenate(both, axis=2).astype(BF)

    out_gin[...] = mgrad[...].astype(F32)
    for r in reversed(range(ROUNDS)):
        p = ROUNDS - 1 - r
        gs = update_back(r + 1, procw[r, 3], procw[r, 4], procw[r, 5])
        gmsg = mm(s.Pc[:, bottom], gs.astype(BF))
        gz = norm_back(gmsg, s.e_msg[r][...].astype(F32), s.e_r[r][:, :1]).astype(BF)
        s.e_msg[r][...] = gz
        dpre = (mt(gz, procw[r, 2]) * swish_grad(s.e_pre[r][...].astype(F32))).astype(BF)
        s.e_pre[r][...] = dpre
        s.bsend[r][...] = tm(s.Ph[...], dpre).astype(BF)
        copies = [halo_copy(s.bsend[r], s.brecv[r], ROUNDS + r, k) for k in range(4)]
        for c in copies:
            c.start()
        mixed[...] = tm(s.Pc[...], s.e_pre[r][...]).astype(BF)
        drecv = mixed[bottom]
        s.drecv[...] = drecv
        out_gin[...] += mt(drecv, procw[r, 1])
        outer_pair(p, 0, (s.lat[r], s.drecv), (s.e_act[r], s.e_msg[r]))
        outer_pair(p, 1, (s.lat[r], s.dgate), (s.u_s[r + 1], s.dgate))
        if p > 0:
            groups[p - 1].add_core()
            groups[p - 1].step()
        for c in copies:
            c.wait()
        dproj = (mixed[top].astype(F32) + tm(s.H[...], s.brecv[r][...])).astype(BF)
        dproj_ref[...] = dproj
        out_gin[...] += mt(dproj, procw[r, 0])
        outer_pair(p, 2, (s.u_hid[r + 1], s.dz), (s.lat[r], dproj_ref))
        groups[p].start_core()

    gs = update_back(0, encw[4], encw[5], encw[6])
    s.gsum[...] = gs.astype(BF)
    s.acc[...] = jnp.zeros((T, L), F32)

    def edge_back(t, _):
        at = pl.ds(pl.multiple_of(t * T, T), T)
        pick = s.Pm[at]
        gmsg = mm(pick, s.gsum[...])
        gz = norm_back(gmsg, s.g_msg[at].astype(F32), s.g_r[at, :1].astype(F32)).astype(BF)
        s.g_msg[at] = gz
        dpre = (mt(gz, encw[3]) * swish_grad(s.g_pre[at].astype(F32))).astype(BF)
        s.g_pre[at] = dpre
        s.acc[...] += tm(pick, dpre)
        s.sendbuf[at] = mt(dpre, encw[1]).astype(BF)
        for q in range(ppt):
            p = t * ppt + q

            @pl.when(p < n - 1)
            def _():
                row_copy(*back_args, p).start()

        return 0

    lax.fori_loop(0, tiles // 2, edge_back, 0)
    groups[1].add_core()
    groups[1].step()
    lax.fori_loop(tiles // 2, tiles, edge_back, 0)
    keep_own(back_args)
    drecv = s.acc[...].astype(BF)
    s.drecv[...] = drecv
    out_gin[...] += mt(drecv, encw[2])
    outer_pair(2, 0, (s.recvbuf, s.g_pre), (s.g_act, s.g_msg))
    outer_pair(2, 1, (mesh_in, s.drecv), (mesh_in, s.dgate))
    outer_pair(2, 2, (s.u_s[0], s.dgate), (s.u_hid[0], s.dz))
    groups[2].start_core()

    s.acc[...] = jnp.zeros((T, L), F32)

    def back_tile(t, _):
        for q in range(ppt):
            p = t * ppt + q

            @pl.when(p < n - 1)
            def _():
                row_copy(*back_args, p).wait_recv()

        at = pl.ds(pl.multiple_of(t * T, T), T)
        s.acc[...] += tm(s.G[at], s.backbuf[at])
        return 0

    lax.fori_loop(0, tiles, back_tile, 0)
    groups[0].step()
    groups[2].add_core()
    groups[2].step()
    dgz = norm_back(s.acc[...], s.grid_norm[...].astype(F32), s.grid_r[:, :1]).astype(BF)
    dgpre = (mt(dgz, encw[0]) * swish_grad(s.emb_pre[...].astype(F32))).astype(BF)
    first = tm(s.emb_act[...], dgz).reshape(ny, nz, nx, per, L)
    second = mm(s.gxp[...], dgpre).T.reshape(ny, nz, nx, per, HALF)
    second = jnp.concatenate([second, jnp.zeros_like(second)], axis=4)
    s.own[3][...] = jnp.concatenate([first, second], axis=3).astype(BF)
    groups[3].start_core()

    def direct_copy(p):
        to = at_offset(p, 1)
        mine = groups[3].half(w.core)
        return pltpu.make_async_remote_copy(
            src_ref=s.own[3].at[w.lat, to // (2 * nx), lax.rem(to // 2, nx), :, mine],
            dst_ref=s.direct.at[p],
            send_sem=s.direct_ss.at[p],
            recv_sem=s.direct_rs.at[p],
            device_id=(w.lat, to),
            device_id_type=MESH,
        )

    def direct_start(p, _):
        direct_copy(p).start()
        return 0

    def direct_wait(p, _):
        direct_copy(p).wait()
        return 0

    groups[3].add_core()
    groups[3].step()
    groups[1].step()
    groups[0].step()
    groups[2].step()
    groups[3].step()
    lax.fori_loop(0, n - 1, direct_start, 0)
    groups[1].step()
    groups[0].start_swap()
    groups[2].step()
    groups[1].start_swap()
    groups[2].start_swap()
    lax.fori_loop(0, n - 1, direct_wait, 0)
    same = s.own[3][w.lat, w.z, w.x, :, groups[3].half(w.core)].astype(F32)
    other = jnp.zeros((2 * per, HALF), F32)
    for p in range(n - 1):
        if STRIDE * (p + 1) % n % 2 == 0:
            same = same + s.direct[p].astype(F32)
        else:
            other = other + s.direct[p].astype(F32)
    s.fin[3][...] = same
    s.swap[3][...] = other
    sent_all(back_args)

    left, right = pl.ds(0, HALF), pl.ds(HALF, HALF)
    for p in range(ROUNDS):
        for k, (a, b) in zip((1, 2, 3, 4, 5, 0), groups[p].finish()):
            out_proc[ROUNDS - 1 - p, k, :, left] = a
            out_proc[ROUNDS - 1 - p, k, :, right] = b
    for k, (a, b) in zip((1, 3, 2, 4, 5, 6), groups[2].finish()):
        out_enc[k, :, left] = a
        out_enc[k, :, right] = b
    last = groups[3].finish()
    out_enc[0, :, left], out_enc[0, :, right] = last[0]
    out_emb[...] = last[1][0][:, :variables]


def hand_over(*refs):
    count = len(refs) // 2
    for k in range(count):
        refs[count + k][...] = refs[k][...]


def on_device(
    cfg,
    grid_x,
    mesh_in,
    mesh_grad,
    embed_in,
    enc_weights,
    proc_weights,
    g2m_grid,
    g2m_mesh,
    mesh_send,
    mesh_recv,
    halo_idx,
):
    n = lax.axis_size("lon")
    count = g2m_grid.shape[0]
    cap = (count + n - 1) // n
    variables = grid_x.shape[1]
    mine = L // (cfg[0] * cfg[1] * cfg[2]) // 2
    plan = scratch_plan(cfg, n, n * cap, mesh_send.shape[0])
    vmem = pl.BlockSpec(memory_space=pltpu.VMEM)
    smem = pl.BlockSpec(memory_space=pltpu.SMEM)
    hbm = pl.BlockSpec(memory_space=pl.ANY)
    shapes = (
        jax.ShapeDtypeStruct((T, L), BF),
        jax.ShapeDtypeStruct((T, L), F32),
        jax.ShapeDtypeStruct((7, mine, L), F32),
        jax.ShapeDtypeStruct((ROUNDS, 6, mine, L), F32),
        jax.ShapeDtypeStruct((mine, variables), F32),
    )
    results = pl.pallas_call(
        functools.partial(kernel, cfg, n, cap, plan),
        out_shape=shapes,
        in_specs=[vmem] * 4 + [hbm] * 2 + [vmem] * 2 + [smem] * 3,
        out_specs=(vmem,) * 5,
        scratch_shapes=leaves(plan),
        compiler_params=pltpu.CompilerParams(
            collective_id=0, has_side_effects=True, vmem_limit_bytes=63 * 1024 * 1024
        ),
    )(
        grid_x.T,
        mesh_in,
        mesh_grad,
        embed_in,
        enc_weights,
        proc_weights,
        g2m_mesh.reshape(1, count),
        g2m_grid.reshape(1, count),
        mesh_send,
        mesh_recv,
        halo_idx.reshape(4),
    )
    latent, grad_in, enc, proc, emb_t = pl.pallas_call(
        hand_over,
        out_shape=shapes,
        in_specs=[vmem] * 5,
        out_specs=(vmem,) * 5,
    )(*results)
    return latent, grad_in, enc, proc, emb_t.T


def solution(mesh):
    n = mesh.shape["lon"]
    nx = 4 if n == 32 else 2
    cfg = (mesh.shape["lat"], n // (2 * nx), nx)
    return jax.shard_map(
        functools.partial(on_device, cfg),
        mesh=mesh,
        in_specs=(
            P(("lat", "lon"), None),
            P(("lat", "lon"), None),
            P(("lat", "lon"), None),
            P(),
            P(),
            P(),
            P(("lat", "lon")),
            P(("lat", "lon")),
            P(("lat", "lon")),
            P(("lat", "lon")),
            P(("lat", "lon"), None, None),
        ),
        out_specs=(
            P(("lat", "lon"), None),
            P(("lat", "lon"), None),
            P(None, ("lat", "lon"), None),
            P(None, None, ("lat", "lon"), None),
            P(None, ("lat", "lon")),
        ),
        check_vma=False,
    )
```
